256 devices in a mesh: dp: 8 (over z), ctx: 32 (over x, y, core).
Axes of the slice: x: 4, y: 4, z: 8, core: 2. Of those that a mesh axis runs over, the one named last changes fastest.
Arguments:
- queries: bfloat16 [8, 8192, 4096], P('dp', 'ctx'), may hold values from -64 to 64
- latent_kv: bfloat16 [8, 512, 8192], P('dp', 'ctx'), may hold values from -8 to 8
- media: int32 [8, 128], P('dp', 'ctx'), may hold values from 0 to 7, as said below
- gate: float32 [32], replicated, may hold values from 0.3 to 1.5
- grad_out: bfloat16 [8, 8192, 4096], P('dp', 'ctx'), may hold values from -16 to 16
Outputs:
- attended: bfloat16 [8, 8192, 4096], P('dp', 'ctx')
- query_grad: bfloat16 [8, 8192, 4096], P('dp', 'ctx')
- latent_grad: bfloat16 [8, 512, 8192], P('dp', 'ctx')
- gate_grad: float32 [32], replicated
The draws below stay inside these ranges and needn't reach their ends.
Inputs may be any that keep to these rules, and one draw needn't show every extreme that they name: Along each sequence the media index never falls; one image of each sequence is named by exactly 121 consecutive blocks and every other image by exactly one block.
All inputs are finite; a program needn't handle non-finite values.
Results may differ from the reference program's by a relative error of at most 0.0059.
Values may be sent and summed in bfloat16 or wider, within the bound.
No kernel may reach another device: no remote copies, remote signals or barrier semaphores. Data moves between devices by JAX's collectives and lax.ppermute only.
A program may use at most 128 MiB of HBM per device.

```python
import jax
import jax.numpy as jnp
from jax import lax

H = 32
HS = 128
NLAT = 64
BLK = 64
F = 4096
BATCH = 8
LENGTH = 8192
NBLK = 128
IMAGES = 8
MOST = 121


def draw_queries(key, part):
    key = jax.random.fold_in(key, 2)
    shape = (BATCH, LENGTH, F)
    values = jnp.clip(jax.random.normal(key, shape, jnp.float32), -6.0, 6.0)
    return values.astype(jnp.bfloat16)


def draw_latent_kv(key, part):
    key = jax.random.fold_in(key, 1)
    shape = (BATCH, IMAGES * NLAT, 2 * F)
    values = jnp.clip(jax.random.normal(key, shape, jnp.float32), -6.0, 6.0)
    return values.astype(jnp.bfloat16)


def draw_media(key, part):
    key = jax.random.fold_in(key, 4)
    leading = jax.random.randint(key, (BATCH, 1), 0, IMAGES).astype(jnp.int32)
    block = jnp.arange(NBLK, dtype=jnp.int32)[None, :]
    after = block - MOST + 1
    inside = jnp.broadcast_to(leading, (BATCH, NBLK))
    media = jnp.where(block < leading, block, jnp.where(block < leading + MOST, inside, after))
    return media.astype(jnp.int32)


def draw_grad_out(key, part):
    key = jax.random.fold_in(key, 3)
    shape = (BATCH, LENGTH, F)
    along = 0.6 + 1.2 * jnp.arange(LENGTH, dtype=jnp.float32) / (LENGTH - 1)
    across = 0.6 + 1.2 * jnp.arange(BATCH, dtype=jnp.float32) / max(BATCH - 1, 1)
    base = jnp.clip(jax.random.normal(key, shape, jnp.float32), -4.0, 4.0)
    return (base * along[None, :, None] * across[:, None, None]).astype(jnp.bfloat16)


def setup_inputs(seed: int = 0) -> dict:
    splits = jax.random.split(jax.random.key(seed), 6)
    queries = draw_queries(jax.random.fold_in(splits[5], 71), 0)
    latent_kv = draw_latent_kv(jax.random.fold_in(splits[5], 71), 0)
    media = draw_media(jax.random.fold_in(splits[5], 71), 0)
    gate = jnp.clip(jax.random.uniform(splits[3], (H,), jnp.float32, 0.3, 1.5), 0.3, 1.5)
    grad_out = draw_grad_out(jax.random.fold_in(splits[5], 71), 0)
    return {"queries": queries, "latent_kv": latent_kv, "media": media, "gate": gate, "grad_out": grad_out}


def rounded(value):
    return lax.optimization_barrier(value.astype(jnp.bfloat16)).astype(jnp.float32)


def one_sequence(items):
    queries, latent_kv, media, gate, grad_out = items
    scale = HS ** -0.5
    table = latent_kv.reshape(IMAGES, NLAT, 2 * F)
    chosen = jnp.take(table, media, axis=0)
    keys = chosen[..., :F].reshape(NBLK, NLAT, H, HS).astype(jnp.float32)
    values = chosen[..., F:].reshape(NBLK, NLAT, H, HS).astype(jnp.float32)
    query_blocks = queries.reshape(NBLK, BLK, H, HS).astype(jnp.float32)
    scores = jnp.einsum("bthd,bjhd->bhtj", query_blocks, keys) * scale
    probs = jax.nn.softmax(scores, axis=-1)
    probs_b = rounded(probs)
    mix = jnp.einsum("bhtj,bjhd->bthd", probs_b, values)
    tgate = jnp.tanh(gate)[None, None, :, None]
    attended = (tgate * mix).astype(jnp.bfloat16).reshape(LENGTH, F)
    upstream = grad_out.reshape(NBLK, BLK, H, HS).astype(jnp.float32)
    gate_part = jnp.einsum("bthd,bthd->h", upstream, mix, precision=lax.Precision.HIGHEST)
    dmix = rounded(tgate * upstream)
    dprob = jnp.einsum("bthd,bjhd->bhtj", dmix, values)
    inner = jnp.sum(probs * dprob, axis=-1, keepdims=True)
    dscore = rounded(probs * (dprob - inner))
    query_grad = (jnp.einsum("bhtj,bjhd->bthd", dscore, keys) * scale).astype(jnp.bfloat16).reshape(LENGTH, F)
    key_part = jnp.einsum("bhtj,bthd->bjhd", dscore, query_blocks) * scale
    value_part = jnp.einsum("bhtj,bthd->bjhd", probs_b, dmix)
    terms = jnp.concatenate([key_part.reshape(NBLK, NLAT, F), value_part.reshape(NBLK, NLAT, F)], axis=-1)
    latent_sum = jax.ops.segment_sum(terms, media, num_segments=IMAGES)
    latent_grad = latent_sum.reshape(IMAGES * NLAT, 2 * F).astype(jnp.bfloat16)
    return attended, query_grad, latent_grad, gate_part


def reference(queries, latent_kv, media, gate, grad_out):
    gates = jnp.broadcast_to(gate[None, :], (BATCH, H))
    attended, query_grad, latent_grad, gate_parts = lax.map(
        one_sequence, (queries, latent_kv, media, gates, grad_out))
    gate_sum = jnp.sum(gate_parts, axis=0)
    tanh_gate = jnp.tanh(gate)
    gate_grad = (1.0 - tanh_gate * tanh_gate) * gate_sum
    return attended, query_grad, latent_grad, gate_grad
```

```python
import functools

import jax
import jax.numpy as jnp
import numpy as np
from jax import lax
from jax.experimental import pallas as pl
from jax.experimental.pallas import tpu as pltpu
from jax.sharding import Mesh
from jax.sharding import PartitionSpec as P

CTX = ("x", "yh", "yl", "c")
IMG = ("x", "yh")
NLAT = 64
HEADS = 32
HS = 128
GRP = 8
COLS = GRP * HS
WIDE = COLS + 128
SCALE = HS**-0.5

NEAR0 = (2, 8, 6, 24)
NEAR1 = (28, 22, 6, 24)
OWNER0 = [NEAR0[j % 4] + j // 4 for j in range(8)]
OWNER1 = [NEAR1[j % 4] + j // 4 for j in range(8)]
IMAGE_OF = [0] * 32
for _j in range(8):
    IMAGE_OF[OWNER0[_j]] = _j
    IMAGE_OF[OWNER1[_j]] = _j
STEP0 = (0, 1, 2, 3)
STEP1 = (0, 1, 3, 2)


def pairs_out(s):
    a, b = NEAR0[STEP0[s]], NEAR1[STEP1[s]]
    return [(0, a), (1, a + 1), (30, b), (31, b + 1)]


def pairs_back(s):
    return [(b, a) for a, b in pairs_out(s)]


def nt(a, b):
    return lax.dot_general(a, b, (((1,), (1,)), ((), ())), preferred_element_type=jnp.float32)


def tn(a, b):
    return lax.dot_general(a, b, (((0,), (0,)), ((), ())), preferred_element_type=jnp.float32)


def nn(a, b):
    return lax.dot_general(a, b, (((1,), (0,)), ((), ())), preferred_element_type=jnp.float32)


def spread_kernel(lead, got, out):
    sel = got[lead[0]]
    for p in range(32):
        out[p, 0] = sel
        out[p, 1] = got[IMAGE_OF[p]]


def one_head(q, g, k, v, tg, keep):
    s = nt(k, q) * SCALE
    e = jnp.exp(s - jnp.max(s, axis=0, keepdims=True))
    p = e * (keep / jnp.sum(e, axis=0, keepdims=True))
    pb = p.astype(jnp.bfloat16)
    mix = tn(pb, v)
    gf = g.astype(jnp.float32)
    gsum = jnp.sum(gf * mix, axis=0, keepdims=True)
    dm = (tg * gf).astype(jnp.bfloat16)
    dp = nt(v, dm)
    inner = jnp.sum(p * dp, axis=0, keepdims=True)
    ds = (p * (dp - inner)).astype(jnp.bfloat16)
    dq = tn(ds, k) * SCALE
    dk = nn(ds, q) * SCALE
    dv = nn(pb, dm)
    bf = jnp.bfloat16
    return (tg * mix).astype(bf), dq.astype(bf), dk.astype(bf), dv.astype(bf), gsum


def attention_kernel(flags, tg, q, g, kv, x0, x1, x2, x3, o, dq, xo, pay, xbuf, gacc, sem):
    c = pl.program_id(0)
    tokens = q.shape[0]
    active = flags[4] == 1

    @pl.when(c == 0)
    def _():
        gacc[...] = jnp.zeros_like(gacc)
        for n, x in enumerate((x0, x1, x2, x3)):

            @pl.when(active & (flags[5] == n))
            def _():
                pltpu.make_async_copy(x, xbuf, sem).start()

    block = lax.broadcasted_iota(jnp.int32, (1, tokens), 1) // (tokens // 4)
    keep = jnp.zeros((1, tokens), jnp.float32)
    for b in range(4):
        keep = jnp.where((block == b) & (flags[b] == 1), 1.0, keep)

    def work(slot, qf, gf, of, dqf, keep):
        for n in range(GRP):
            cols = slice(n * HS, n * HS + HS)
            h = c * GRP + n
            k = kv[0, 0, :, slot, :, cols].reshape(NLAT, HS)
            v = kv[1, 0, :, slot, :, cols].reshape(NLAT, HS)
            ob, dqb, dkb, dvb, gsum = one_head(qf(cols), gf(cols), k, v, tg[h], keep)
            of(cols, ob)
            dqf(cols, dqb)
            rows = slice(16 * slot, 16 * slot + 16)
            pay[0, c, :, rows, cols] = dkb.reshape(4, 16, HS)
            pay[1, c, :, rows, cols] = dvb.reshape(4, 16, HS)
            gacc[pl.ds(h, 1), :] += gsum

    def put(ref, *lead):
        def f(cols, val):
            ref[(*lead, slice(None), cols)] = val

        return f

    work(0, lambda s: q[:, s], lambda s: g[:, s], put(o), put(dq), keep)

    @pl.when(active)
    def _():
        @pl.when(c == 0)
        def _():
            pltpu.make_async_copy(x0, xbuf, sem).wait()

        work(
            1,
            lambda s: xbuf[0, c, :, s],
            lambda s: xbuf[1, c, :, s],
            put(xo, 0),
            put(xo, 1),
            jnp.ones((1, NLAT), jnp.float32),
        )

    @pl.when(c == pl.num_programs(0) - 1)
    def _():
        gs = jnp.sum(gacc[...].T, axis=0, keepdims=True)
        hi = gs.astype(jnp.bfloat16).astype(jnp.float32)
        mid = (gs - hi).astype(jnp.bfloat16).astype(jnp.float32)
        lo = gs - hi - mid
        row = lax.broadcasted_iota(jnp.int32, (16, HS), 0)
        val = jnp.where(row == 0, hi, jnp.where(row == 1, mid, jnp.where(row == 2, lo, 0.0)))
        val = val.astype(jnp.bfloat16)
        for a in range(2):
            for b in range(4):
                for r in range(4):
                    pay[a, b, r, 0:16, COLS:WIDE] = val


def collect_kernel(lead, got, out, gsum):
    total = jnp.zeros((16, COLS), jnp.float32)
    gates = jnp.zeros((16, 128), jnp.float32)
    for p in range(32):
        total += got[p, 0:16, 0:COLS].astype(jnp.float32)
        gates += got[p, 0:16, COLS:WIDE].astype(jnp.float32)
    gsum[...] = jnp.sum(gates, axis=0, keepdims=True)
    first = lead[0]
    for j in range(8):

        @pl.when(j < first)
        def _():
            out[j] = got[OWNER0[j], 16:32, 0:COLS]

        @pl.when(j > first)
        def _():
            out[j] = got[OWNER1[j], 16:32, 0:COLS]

        @pl.when(j == first)
        def _():
            out[j] = total.astype(jnp.bfloat16)


def merge_kernel(flags, o_in, dq_in, r0, r1, r2, r3, o, dq, sem):
    del o_in, dq_in
    for s, r in enumerate((r0, r1, r2, r3)):
        k = flags[8 + s]
        rows = pl.ds(pl.multiple_of(k * NLAT, NLAT), NLAT)

        @pl.when(flags[12 + s] == 1)
        def _():
            first = pltpu.make_async_copy(r.at[0], o.at[rows], sem.at[0])
            second = pltpu.make_async_copy(r.at[1], dq.at[rows], sem.at[1])
            first.start()
            second.start()
            first.wait()
            second.wait()


VM = pl.BlockSpec(memory_space=pltpu.VMEM)
SM = pl.BlockSpec(memory_space=pltpu.SMEM)
ANY = pl.BlockSpec(memory_space=pl.ANY)
LIMIT = 48 * 1024 * 1024


def body(queries, latent_kv, media, gate, grad_out):
    bf = jnp.bfloat16
    q, g = queries[0], grad_out[0]
    tokens, width = q.shape
    ctx = lax.axis_index(CTX)
    core = lax.axis_index("c")
    mine = media[0]
    other = lax.ppermute(mine, "c", [(0, 1), (1, 0)])
    early = jnp.where(core == 0, mine, other)
    late = jnp.where(core == 0, other, mine)
    lead = jnp.where(ctx < 2, late[3], early[0])

    qb = q.reshape(4, NLAT, width)
    gb = g.reshape(4, NLAT, width)
    high = ctx >= 16
    sent = []
    for s in range(4):
        k = jnp.where(high, STEP1[s], STEP0[s])
        both = jnp.stack([qb[k], gb[k]])
        both = both.reshape(2, NLAT, 4, COLS).transpose(0, 2, 1, 3)
        sent.append(lax.ppermute(both, CTX, pairs_out(s)))

    image = jnp.asarray(np.array(IMAGE_OF, np.int32))[ctx]
    is0 = np.isin(np.arange(32), OWNER0)
    is1 = np.isin(np.arange(32), OWNER1)
    from0 = jnp.asarray(is0)[ctx] & (image < lead)
    from1 = jnp.asarray(is1)[ctx] & (image > lead)
    step0 = np.zeros(32, np.int32)
    step1 = np.zeros(32, np.int32)
    for s in range(4):
        for core_ in range(2):
            step0[NEAR0[STEP0[s]] + core_] = s
            step1[NEAR1[STEP1[s]] + core_] = s
    source = jnp.where(from0, jnp.asarray(step0)[ctx], jnp.asarray(step1)[ctx])
    main = (mine == lead).astype(jnp.int32)
    hot = (ctx < 2) | (ctx >= 30)
    order = jnp.where(high, jnp.array(STEP1, jnp.int32), jnp.array(STEP0, jnp.int32))
    odd = jnp.where(hot, 1 - jnp.where(high, main[np.array(STEP1)], main[np.array(STEP0)]), 0)
    zero = jnp.zeros((2,), jnp.int32)
    flags = jnp.concatenate(
        [main, (from0 | from1).astype(jnp.int32)[None], source[None], zero, order, odd]
    ).astype(jnp.int32)
    lead1 = lead[None]

    chunks = latent_kv[0].reshape(16, 8, COLS).transpose(1, 0, 2)
    mixed = lax.all_to_all(chunks, IMG, 0, 0, tiled=True)
    spread = pl.pallas_call(
        spread_kernel,
        out_shape=jax.ShapeDtypeStruct((32, 2, 16, COLS), bf),
        in_specs=[SM, VM],
        out_specs=VM,
        name="spread",
    )(lead1, mixed)
    kv = lax.all_to_all(spread, CTX, 0, 0, tiled=True).reshape(2, 4, 4, 2, 16, COLS)

    tanh_gate = jnp.tanh(gate)
    wide = pl.BlockSpec((tokens, COLS), lambda c: (0, c))
    o, dq, xo, pay = pl.pallas_call(
        attention_kernel,
        grid=(4,),
        out_shape=[
            jax.ShapeDtypeStruct((tokens, width), bf),
            jax.ShapeDtypeStruct((tokens, width), bf),
            jax.ShapeDtypeStruct((2, NLAT, width), bf),
            jax.ShapeDtypeStruct((2, 4, 4, 32, WIDE), bf),
        ],
        in_specs=[
            SM,
            SM,
            wide,
            wide,
            pl.BlockSpec((2, 1, 4, 2, 16, COLS), lambda c: (0, c, 0, 0, 0, 0)),
            ANY,
            ANY,
            ANY,
            ANY,
        ],
        out_specs=[
            wide,
            wide,
            pl.BlockSpec((2, NLAT, COLS), lambda c: (0, 0, c)),
            pl.BlockSpec((2, 4, 4, 32, WIDE), lambda c: (0, 0, 0, 0, 0)),
        ],
        scratch_shapes=[
            pltpu.VMEM((2, 4, NLAT, COLS), bf),
            pltpu.VMEM((128, HS), jnp.float32),
            pltpu.SemaphoreType.DMA,
        ],
        compiler_params=pltpu.CompilerParams(vmem_limit_bytes=LIMIT),
        name="attention",
    )(flags, tanh_gate, q, g, kv, *sent)

    back = [lax.ppermute(xo, CTX, pairs_back(s)) for s in range(4)]
    parts = lax.all_to_all(pay.reshape(32, 32, WIDE), CTX, 0, 0, tiled=True)
    owned, gsum = pl.pallas_call(
        collect_kernel,
        out_shape=[
            jax.ShapeDtypeStruct((8, 16, COLS), bf),
            jax.ShapeDtypeStruct((1, 128), jnp.float32),
        ],
        in_specs=[SM, VM],
        out_specs=[VM, VM],
        compiler_params=pltpu.CompilerParams(vmem_limit_bytes=LIMIT),
        name="collect",
    )(lead1, parts)
    gates = gsum
    for n in range(1, 8):
        gates = gates + lax.ppermute(gsum, "dp", [(s, (s + n) % 8) for s in range(8)])
    final = lax.all_to_all(owned, IMG, 0, 0, tiled=True)
    latent_grad = final.transpose(1, 0, 2).reshape(1, 16, 8 * COLS)
    o, dq = pl.pallas_call(
        merge_kernel,
        out_shape=[
            jax.ShapeDtypeStruct((tokens, width), bf),
            jax.ShapeDtypeStruct((tokens, width), bf),
        ],
        in_specs=[SM] + [ANY] * 6,
        out_specs=[ANY, ANY],
        scratch_shapes=[pltpu.SemaphoreType.DMA((2,))],
        input_output_aliases={1: 0, 2: 1},
        name="merge",
    )(flags, o, dq, *back)
    gate_grad = (1.0 - tanh_gate * tanh_gate) * gates[0, :HEADS]
    return o[None], dq[None], latent_grad, gate_grad


def solution(mesh):
    fine = Mesh(mesh.devices.reshape(8, 4, 2, 2, 2), ("dp", "x", "yh", "yl", "c"))
    wide = P("dp", CTX, None)
    return jax.shard_map(
        body,
        mesh=fine,
        in_specs=(wide, wide, P("dp", CTX), P(), wide),
        out_specs=(wide, wide, wide, P()),
        check_vma=False,
    )
```

```python
import jax
import jax.numpy as jnp
from jax import lax
from jax.experimental import pallas as pl
from jax.experimental.pallas import tpu as pltpu
from jax.sharding import Mesh
from jax.sharding import PartitionSpec as P

CTX = ("x", "yh", "yl", "c")
CHIP = ("x", "yh", "yl")
IMG = ("x", "yh")
NLAT = 64
HEADS = 32
HS = 128
GRP = 8
BATCH = 4
COLS = GRP * HS
WIDE = COLS + 128
QUART = 16
SCALE = HS**-0.5
BF = jnp.bfloat16
F32 = jnp.float32

NEAR0 = (2, 8, 6, 24)
NEAR1 = (28, 22, 6, 24)
WORKER0 = [NEAR0[j % 4] + j // 4 for j in range(8)]
WORKER1 = [NEAR1[j % 4] + j // 4 for j in range(8)]
STEP0 = (0, 1, 2, 3)
STEP1 = (0, 1, 3, 2)


def block_pairs(s):
    a, b = NEAR0[STEP0[s]], NEAR1[STEP1[s]]
    return [(0, a), (1, a + 1), (30, b), (31, b + 1)]


def latent_pairs(s):
    first = [(4 * j + s, WORKER0[j]) for j in range(8)]
    second = [(4 * j + (s + 1) % 4, WORKER1[j]) for j in range(8) if WORKER1[j] != WORKER0[j]]
    return first + second


def back(pairs):
    return [(b, a) for a, b in pairs]


def nt(a, b):
    return lax.dot_general(a, b, (((1,), (1,)), ((), ())), preferred_element_type=F32)


def tn(a, b):
    return lax.dot_general(a, b, (((0,), (0,)), ((), ())), preferred_element_type=F32)


def nn(a, b):
    return lax.dot_general(a, b, (((1,), (0,)), ((), ())), preferred_element_type=F32)


def pick(cases, default):
    out = jnp.int32(default)
    for cond, value in cases:
        out = jnp.where(cond, jnp.int32(value), out)
    return out


def step_block(ctx, s):
    return jnp.where(ctx >= 16, jnp.int32(STEP1[s]), jnp.int32(STEP0[s]))


def chunk_kernel(src, dst):
    for i in range(8):
        dst[i] = src[:, i * COLS : (i + 1) * COLS]


def pack_kernel(ctx_ref, q, g, d0, d1, d2, d3, buf, sems):
    ctx = ctx_ref[0]

    @pl.when((ctx < 2) | (ctx >= 30))
    def _():
        loads = []
        for s in range(4):
            rows = pl.ds(pl.multiple_of(step_block(ctx, s) * NLAT, NLAT), NLAT)
            for a, ref in enumerate((q, g)):
                copy = pltpu.make_async_copy(ref.at[rows], buf.at[s, a], sems.at[0, s, a])
                copy.start()
                loads.append(copy)
        stores = []
        for s, d in enumerate((d0, d1, d2, d3)):
            for a in range(2):
                loads[2 * s + a].wait()
                copy = pltpu.make_async_copy(buf.at[s, a], d.at[a], sems.at[1, s, a])
                copy.start()
                stores.append(copy)
        for copy in stores:
            copy.wait()


def spread_kernel(ids, got, dst):
    sel = got[ids[1]]
    for p in range(16):
        dst[p] = sel


def heads_side_by_side(items):
    s = [nt(k, q) for q, g, k, v, t, keep in items]
    gf = [g.astype(F32) for q, g, k, v, t, keep in items]
    dm = [(it[4] * f).astype(BF) for it, f in zip(items, gf)]
    dp = [nt(it[3], d) for it, d in zip(items, dm)]
    e = [jnp.exp((x - jnp.max(x, axis=0, keepdims=True)) * SCALE) for x in s]
    p = [x * (it[5] / jnp.sum(x, axis=0, keepdims=True)) for it, x in zip(items, e)]
    pb = [x.astype(BF) for x in p]
    mix = [tn(x, it[3]) for it, x in zip(items, pb)]
    inner = [jnp.sum(a * b, axis=0, keepdims=True) for a, b in zip(p, dp)]
    ds = [(a * (b - c)).astype(BF) for a, b, c in zip(p, dp, inner)]
    dv = [nn(a, b) for a, b in zip(pb, dm)]
    dq = [tn(a, it[2]) * SCALE for it, a in zip(items, ds)]
    dk = [nn(a, it[0]) * SCALE for it, a in zip(items, ds)]
    gs = [jnp.sum(a * b, axis=0, keepdims=True) for a, b in zip(gf, mix)]
    out = [(it[4] * m).astype(BF) for it, m in zip(items, mix)]
    return list(zip(out, [x.astype(BF) for x in dq], dk, dv, gs))


def split3(x):
    hi = x.astype(BF).astype(F32)
    mid = (x - hi).astype(BF).astype(F32)
    lo = x - hi - mid
    row = lax.broadcasted_iota(jnp.int32, (16, x.shape[1]), 0)
    val = jnp.where(row == 0, hi, jnp.where(row == 1, mid, jnp.where(row == 2, lo, 0.0)))
    return val.astype(BF)


def attention_kernel(
    ids, tg, q, g, mine, other, l0, l1, l2, l3, x0, x1, x2, x3,
    o, dq, xo, pay, opay, y0, y1, y2, y3, gate, xbuf, gacc, sem,
):
    c = pl.program_id(0)
    tokens = q.shape[0]
    width = o.shape[1] * 4
    ctx, lead = ids[0], ids[1]
    latents = (l0, l1, l2, l3)
    grads = (y0, y1, y2, y3)
    from0 = [(ctx == WORKER0[j]) & (lead > j) for j in range(8)]
    from1 = [(ctx == WORKER1[j]) & (lead < j) for j in range(8)]
    cases = [(from0[j], STEP0.index(j % 4)) for j in range(8)]
    cases += [(from1[j], STEP1.index(j % 4)) for j in range(8)]
    source = pick(cases, -1)

    @pl.when(c == 0)
    def _():
        gacc[...] = jnp.zeros_like(gacc)
        for n, x in enumerate((x0, x1, x2, x3)):

            @pl.when(source == n)
            def _():
                copy = pltpu.make_async_copy(x, xbuf, sem)
                copy.start()
                copy.wait()

    block = lax.broadcasted_iota(jnp.int32, (1, tokens), 1) // (tokens // 4)
    keep = jnp.zeros((1, tokens), F32)
    for b in range(4):
        keep = jnp.where((block == b) & (ids[2 + b] == lead), 1.0, keep)
    ones = jnp.ones((1, NLAT), F32)

    def work(extra):
        for first in range(0, GRP, BATCH):
            items, heads = [], range(first, first + BATCH)
            for n in heads:
                cols = slice(n * HS, n * HS + HS)
                t = tg[c * GRP + n]
                k = [ref[0, 0, y, :, cols] for ref in (mine, other) for y in range(2)]
                v = [ref[1, 0, y, :, cols] for ref in (mine, other) for y in range(2)]
                k, v = jnp.concatenate(k, axis=0), jnp.concatenate(v, axis=0)
                items.append((q[:, cols], g[:, cols], k, v, t, keep))
                if extra:
                    wk = pl.ds(pl.multiple_of(c * COLS + n * HS, HS), HS)
                    wv = pl.ds(pl.multiple_of(width + c * COLS + n * HS, HS), HS)
                    k = jnp.concatenate([ref[:, wk] for ref in latents], axis=0)
                    v = jnp.concatenate([ref[:, wv] for ref in latents], axis=0)
                    items.append((xbuf[0, :, wk], xbuf[1, :, wk], k, v, t, ones))
            done = heads_side_by_side(items)
            for n in heads:
                cols = slice(n * HS, n * HS + HS)
                ob, dqb, dk, dv, gs = done.pop(0)
                o[:, cols] = ob
                dq[:, cols] = dqb
                for kv, d in enumerate((dk, dv)):
                    for y in range(2):
                        at = kv * 8 + c * 2 + y
                        pay[at, :, cols] = d[y * QUART : (y + 1) * QUART]
                        opay[at, :, cols] = d[(2 + y) * QUART : (3 + y) * QUART].astype(BF)
                if extra:
                    wk = pl.ds(pl.multiple_of(c * COLS + n * HS, HS), HS)
                    wv = pl.ds(pl.multiple_of(width + c * COLS + n * HS, HS), HS)
                    ob, dqb, dk, dv, gx = done.pop(0)
                    xo[0, :, cols] = ob
                    xo[1, :, cols] = dqb
                    for s in range(4):
                        grads[s][:, wk] = dk[s * QUART : (s + 1) * QUART].astype(BF)
                        grads[s][:, wv] = dv[s * QUART : (s + 1) * QUART].astype(BF)
                    gs = gs + gx
                gacc[pl.ds(c * GRP + n, 1), :] = gs

    @pl.when(source >= 0)
    def _():
        work(True)

    @pl.when(source < 0)
    def _():
        work(False)

    @pl.when(c == pl.num_programs(0) - 1)
    def _():
        gs = jnp.sum(gacc[...].T, axis=0, keepdims=True)
        gate[...] = gs
        opay[16] = jnp.zeros((QUART, COLS), BF)
        opay[16, :, 0:HS] = split3(gs)


def pair_kernel(pay, got, gate, dst):
    for d in range(16):
        dst[d, :, 0:COLS] = (pay[d] + got[d].astype(F32)).astype(BF)
    other = jnp.sum(got[16, :, 0:HS].astype(F32), axis=0, keepdims=True)
    val = split3(gate[...] + other)
    for d in range(16):
        dst[d, :, COLS:WIDE] = val


def collect_kernel(got, dst, gate):
    total = got[0].astype(F32)
    for p in range(1, 16):
        total += got[p].astype(F32)
    gate[...] = jnp.sum(total[:, COLS:WIDE], axis=0, keepdims=True)
    val = total[:, 0:COLS].astype(BF)
    for j in range(8):
        dst[j] = val


def assemble_kernel(ids, got, y0, y1, y2, y3, dst):
    ctx, lead = ids[0], ids[1]
    image, quarter = ctx // 4, ctx % 4
    shared = (image % 4) >= 2
    step = jnp.where((image < lead) | shared, quarter, (quarter + 3) % 4)

    @pl.when(image == lead)
    def _():
        for i in range(8):
            dst[:, i * COLS : (i + 1) * COLS] = got[i]

    for s, y in enumerate((y0, y1, y2, y3)):

        @pl.when((image != lead) & (step == s))
        def _():
            dst[...] = y[...]


def merge_kernel(ids, o_in, dq_in, r0, r1, r2, r3, o, dq, buf, sems):
    del o_in, dq_in
    ctx, lead = ids[0], ids[1]

    @pl.when((ctx < 2) | (ctx >= 30))
    def _():
        for s, r in enumerate((r0, r1, r2, r3)):
            odd = ids[2 + step_block(ctx, s)] != lead

            @pl.when(odd)
            def _():
                pltpu.make_async_copy(r, buf.at[s], sems.at[s, 0]).start()

        for s, r in enumerate((r0, r1, r2, r3)):
            k = step_block(ctx, s)
            odd = ids[2 + k] != lead
            rows = pl.ds(pl.multiple_of(k * NLAT, NLAT), NLAT)

            @pl.when(odd)
            def _():
                pltpu.make_async_copy(r, buf.at[s], sems.at[s, 0]).wait()
                pltpu.make_async_copy(buf.at[s, 0], o.at[rows], sems.at[s, 1]).start()
                pltpu.make_async_copy(buf.at[s, 1], dq.at[rows], sems.at[s, 2]).start()

        for s in range(4):
            k = step_block(ctx, s)
            odd = ids[2 + k] != lead
            rows = pl.ds(pl.multiple_of(k * NLAT, NLAT), NLAT)

            @pl.when(odd)
            def _():
                pltpu.make_async_copy(buf.at[s, 0], o.at[rows], sems.at[s, 1]).wait()
                pltpu.make_async_copy(buf.at[s, 1], dq.at[rows], sems.at[s, 2]).wait()


VM = pl.BlockSpec(memory_space=pltpu.VMEM)
SM = pl.BlockSpec(memory_space=pltpu.SMEM)
ANY = pl.BlockSpec(memory_space=pl.ANY)
LIMIT = 48 * 1024 * 1024


def shape(*dims, dtype=BF):
    return jax.ShapeDtypeStruct(dims, dtype)


def call(kernel, name, out_shape, in_specs, out_specs, **more):
    params = pltpu.CompilerParams(vmem_limit_bytes=LIMIT)
    return pl.pallas_call(
        kernel,
        name=name,
        out_shape=out_shape,
        in_specs=in_specs,
        out_specs=out_specs,
        compiler_params=params,
        **more,
    )


def body(queries, latent_kv, media, gate, grad_out):
    q, g, kv_rows = queries[0], grad_out[0], latent_kv[0]
    tokens, width = q.shape
    ctx = lax.axis_index(CTX)
    core = lax.axis_index("c")
    images = media[0]
    partner = lax.ppermute(images, "c", [(0, 1), (1, 0)])
    last = jnp.where(core == 0, partner, images)[3]
    first = jnp.where(core == 0, images, partner)[0]
    lead = jnp.where(ctx < 2, last, first)
    ids = jnp.concatenate([ctx[None], lead[None], images]).astype(jnp.int32)

    chunks = call(chunk_kernel, "chunk", shape(8, QUART, COLS), [VM], VM)(kv_rows)
    mixed = lax.all_to_all(chunks, IMG, 0, 0, tiled=True)
    packed = call(
        pack_kernel,
        "pack",
        [shape(2, NLAT, width)] * 4,
        [SM, ANY, ANY],
        [ANY] * 4,
        scratch_shapes=[
            pltpu.VMEM((4, 2, NLAT, width), BF),
            pltpu.SemaphoreType.DMA((2, 4, 2)),
        ],
    )(ctx[None].astype(jnp.int32), q, g)
    sent = [lax.ppermute(packed[s], CTX, block_pairs(s)) for s in range(4)]
    lent = [lax.ppermute(kv_rows, CTX, latent_pairs(s)) for s in range(4)]

    spread = call(spread_kernel, "spread", shape(16, QUART, COLS), [SM, VM], VM)(ids, mixed)
    mine = lax.all_to_all(spread, CHIP, 0, 0, tiled=True).reshape(2, 4, 2, QUART, COLS)
    other = lax.ppermute(mine, "c", [(0, 1), (1, 0)])

    tanh_gate = jnp.tanh(gate)
    wide = pl.BlockSpec((tokens, COLS), lambda c: (0, c))
    half = pl.BlockSpec((2, 1, 2, QUART, COLS), lambda c: (0, c, 0, 0, 0))
    o, dq, xo, pay, opay, y0, y1, y2, y3, gpart = call(
        attention_kernel,
        "attention",
        [
            shape(tokens, width),
            shape(tokens, width),
            shape(2, NLAT, width),
            shape(16, QUART, COLS, dtype=F32),
            shape(17, QUART, COLS),
            *[shape(QUART, 2 * width)] * 4,
            shape(1, HS, dtype=F32),
        ],
        [SM, SM, wide, wide, half, half, *[VM] * 4, *[ANY] * 4],
        [wide, wide, pl.BlockSpec((2, NLAT, COLS), lambda c: (0, 0, c)), *[VM] * 7],
        grid=(4,),
        scratch_shapes=[
            pltpu.VMEM((2, NLAT, width), BF),
            pltpu.VMEM((HS, HS), F32),
            pltpu.SemaphoreType.DMA,
        ],
    )(ids, tanh_gate, q, g, mine, other, *lent, *sent)

    theirs = lax.ppermute(opay, "c", [(0, 1), (1, 0)])
    paired = call(pair_kernel, "pair", shape(16, QUART, WIDE), [VM, VM, VM], VM)(
        pay, theirs, gpart
    )
    parts = lax.all_to_all(paired, CHIP, 0, 0, tiled=True)
    ready = [lax.ppermute(xo, CTX, back(block_pairs(s))) for s in range(4)]
    owned = [
        lax.ppermute(y, CTX, back(latent_pairs(s))) for s, y in enumerate((y0, y1, y2, y3))
    ]
    summed, gates = call(
        collect_kernel,
        "collect",
        [shape(8, QUART, COLS), shape(1, HS, dtype=F32)],
        [VM],
        [VM, VM],
    )(parts)
    final = lax.all_to_all(summed, IMG, 0, 0, tiled=True)
    for n in (1, 2, 4):
        gates = gates + lax.ppermute(gates, "dp", [(s, s ^ n) for s in range(8)])
    latent_grad = call(
        assemble_kernel, "assemble", shape(QUART, 2 * width), [SM, *[VM] * 5], VM
    )(ids, final, *owned)
    o, dq = call(
        merge_kernel,
        "merge",
        [shape(tokens, width)] * 2,
        [SM, *[ANY] * 6],
        [ANY, ANY],
        scratch_shapes=[
            pltpu.VMEM((4, 2, NLAT, width), BF),
            pltpu.SemaphoreType.DMA((4, 3)),
        ],
        input_output_aliases={1: 0, 2: 1},
    )(ids, o, dq, *ready)
    gate_grad = (1.0 - tanh_gate * tanh_gate) * gates[0, :HEADS]
    return o[None], dq[None], latent_grad[None], gate_grad


def solution(mesh):
    fine = Mesh(mesh.devices.reshape(8, 4, 2, 2, 2), ("dp", "x", "yh", "yl", "c"))
    wide = P("dp", CTX, None)
    return jax.shard_map(
        body,
        mesh=fine,
        in_specs=(wide, wide, P("dp", CTX), P(), wide),
        out_specs=(wide, wide, wide, P()),
        check_vma=False,
    )
```

```python
import jax
import jax.numpy as jnp
from jax import lax
from jax.experimental import pallas as pl
from jax.experimental.pallas import tpu as pltpu
from jax.sharding import Mesh
from jax.sharding import PartitionSpec as P

CTX = ("x", "yh", "yl", "c")
CHIP = ("x", "yh", "yl")
IMG = ("x", "yh")
NLAT = 64
HEADS = 32
HS = 128
GRP = 8
BATCH = 4
COLS = GRP * HS
WIDE = COLS + 128
QUART = 16
SCALE = HS**-0.5
DEP_CHUNK = 1
DEP_SPREAD = 0
DEP_LENT = 0
GATE_FIRST = 0
BF = jnp.bfloat16
F32 = jnp.float32

BLOCK_PAIRS = (
    [(0, 2), (1, 7), (31, 25)],
    [(0, 8), (1, 25), (30, 22), (31, 7)],
)
WORK = (
    (2, 0, True, 0),
    (8, 1, True, 1),
    (22, 1, False, 1),
    (7, 4, True, 0),
    (7, 4, False, 1),
    (25, 5, True, 1),
    (25, 5, False, 0),
)


def latent_pairs(s):
    pairs = [(2 * (4 + s), 0), (2 * (4 + s) + 1, 30), (2 * (12 + s) + 1, 31)]
    if s < 2:
        pairs.append((2 * (12 + s), 1))
        pairs += [(2 * s, 2), (2 * (2 + s), 8), (2 * (2 + s) + 1, 22)]
        pairs += [(2 * (8 + s), 7), (2 * (10 + s), 25)]
    return pairs


def back(pairs):
    return [(b, a) for a, b in pairs]


def nt(a, b):
    return lax.dot_general(a, b, (((1,), (1,)), ((), ())), preferred_element_type=F32)


def tn(a, b):
    return lax.dot_general(a, b, (((0,), (0,)), ((), ())), preferred_element_type=F32)


def nn(a, b):
    return lax.dot_general(a, b, (((1,), (0,)), ((), ())), preferred_element_type=F32)


def pick(cases, default):
    out = jnp.int32(default)
    for cond, value in cases:
        out = jnp.where(cond, jnp.int32(value), out)
    return out


def step_block(ctx, s):
    return jnp.where(ctx == 31, jnp.int32(1 - s), jnp.int32(s))


def place(here, images, partner):
    ctx = here[0]
    low = ctx % 2 == 0
    last = jnp.where(low, partner[3], images[3])
    first = jnp.where(low, images[0], partner[0])
    return ctx, jnp.where(ctx < 2, last, first)


def chunk_kernel(src, *rest):
    dst, sems = rest[-2:]
    copies = [
        pltpu.make_async_copy(src.at[:, pl.ds(i * COLS, COLS)], dst.at[i], sems.at[i])
        for i in range(8)
    ]
    for copy in copies:
        copy.start()
    for copy in copies:
        copy.wait()


def pack_kernel(here, q, g, d0, d1, buf, sems):
    ctx = here[0]

    @pl.when((ctx < 2) | (ctx >= 30))
    def _():
        loads = []
        for s in range(2):
            rows = pl.ds(pl.multiple_of(step_block(ctx, s) * NLAT, NLAT), NLAT)
            for a, ref in enumerate((q, g)):
                copy = pltpu.make_async_copy(ref.at[rows], buf.at[s, a], sems.at[0, s, a])
                copy.start()
                loads.append(copy)
        stores = []
        for s, d in enumerate((d0, d1)):
            for a in range(2):
                loads[2 * s + a].wait()
                copy = pltpu.make_async_copy(buf.at[s, a], d.at[a], sems.at[1, s, a])
                copy.start()
                stores.append(copy)
        for copy in stores:
            copy.wait()


def half_kernel(own, other, dst):
    dst[0:QUART] = own[...]
    dst[QUART : 2 * QUART] = other[...]


def spread_kernel(here, images, partner, got, *rest):
    dst = rest[-1]
    _, lead = place(here, images, partner)
    sel = got[lead]
    for p in range(16):
        dst[p] = sel


def heads_side_by_side(items):
    s = [nt(k, q) for q, g, k, v, t, keep in items]
    gf = [g.astype(F32) for q, g, k, v, t, keep in items]
    dm = [(it[4] * f).astype(BF) for it, f in zip(items, gf)]
    dp = [nt(it[3], d) for it, d in zip(items, dm)]
    e = [jnp.exp((x - jnp.max(x, axis=0, keepdims=True)) * SCALE) for x in s]
    p = [x * (it[5] / jnp.sum(x, axis=0, keepdims=True)) for it, x in zip(items, e)]
    pb = [x.astype(BF) for x in p]
    mix = [tn(x, it[3]) for it, x in zip(items, pb)]
    inner = [jnp.sum(a * b, axis=0, keepdims=True) for a, b in zip(p, dp)]
    ds = [(a * (b - c)).astype(BF) for a, b, c in zip(p, dp, inner)]
    dv = [nn(a, b) for a, b in zip(pb, dm)]
    dq = [tn(a, it[2]) * SCALE for it, a in zip(items, ds)]
    dk = [nn(a, it[0]) * SCALE for it, a in zip(items, ds)]
    gs = [jnp.sum(a * b, axis=0, keepdims=True) for a, b in zip(gf, mix)]
    out = [(it[4] * m).astype(BF) for it, m in zip(items, mix)]
    return list(zip(out, [x.astype(BF) for x in dq], dk, dv, gs))


def split3(x):
    hi = x.astype(BF).astype(F32)
    mid = (x - hi).astype(BF).astype(F32)
    lo = x - hi - mid
    row = lax.broadcasted_iota(jnp.int32, (16, x.shape[1]), 0)
    val = jnp.where(row == 0, hi, jnp.where(row == 1, mid, jnp.where(row == 2, lo, 0.0)))
    return val.astype(BF)


def attention_kernel(
    here, images, partner, tg, q, g, mine, other, l0, l1, l2, l3, x0, x1,
    o, dq, xo, pay, opay, y0, y1, y2, y3, gate, xbuf, gacc, sem,
):
    c = pl.program_id(0)
    tokens = q.shape[0]
    width = o.shape[1] * 4
    ctx, lead = place(here, images, partner)
    latents = (l0, l1, l2, l3)
    grads = (y0, y1, y2, y3)
    source = pick(
        [((ctx == w) & ((lead > j) if low else (lead < j)), s) for w, j, low, s in WORK], -1
    )
    hot = (ctx < 2) | (ctx >= 30)

    @pl.when(c == 0)
    def _():
        gacc[...] = jnp.zeros_like(gacc)
        for n, x in enumerate((x0, x1)):

            @pl.when(source == n)
            def _():
                copy = pltpu.make_async_copy(x, xbuf, sem)
                copy.start()
                copy.wait()

    block = lax.broadcasted_iota(jnp.int32, (1, tokens), 1) // (tokens // 4)
    keep = jnp.zeros((1, tokens), F32)
    for b in range(4):
        keep = jnp.where((block == b) & (images[b] == lead), 1.0, keep)
    ones = jnp.ones((1, NLAT), F32)
    stays = [jnp.where(images[k] == lead, 0.0, ones) for k in (2, 3)]

    def work(slots):
        for first in range(0, GRP, BATCH):
            items, heads = [], range(first, first + BATCH)
            for n in heads:
                cols = slice(n * HS, n * HS + HS)
                t = tg[c * GRP + n]
                k = [ref[0, 0, y, :, cols] for ref in (mine, other) for y in range(2)]
                v = [ref[1, 0, y, :, cols] for ref in (mine, other) for y in range(2)]
                k, v = jnp.concatenate(k, axis=0), jnp.concatenate(v, axis=0)
                items.append((q[:, cols], g[:, cols], k, v, t, keep))
                wk = pl.ds(pl.multiple_of(c * COLS + n * HS, HS), HS)
                wv = pl.ds(pl.multiple_of(width + c * COLS + n * HS, HS), HS)
                for z in range(slots):
                    k = jnp.concatenate([ref[:, wk] for ref in latents[2 * z : 2 * z + 2]], axis=0)
                    v = jnp.concatenate([ref[:, wv] for ref in latents[2 * z : 2 * z + 2]], axis=0)
                    if slots == 1:
                        items.append((xbuf[0, :, wk], xbuf[1, :, wk], k, v, t, ones))
                    else:
                        rows = slice((2 + z) * NLAT, (3 + z) * NLAT)
                        items.append((q[rows, cols], g[rows, cols], k, v, t, stays[z]))
            done = heads_side_by_side(items)
            for n in heads:
                cols = slice(n * HS, n * HS + HS)
                wk = pl.ds(pl.multiple_of(c * COLS + n * HS, HS), HS)
                wv = pl.ds(pl.multiple_of(width + c * COLS + n * HS, HS), HS)
                ob, dqb, dk, dv, gs = done.pop(0)
                for kv, d in enumerate((dk, dv)):
                    for y in range(2):
                        at = kv * 8 + c * 2 + y
                        pay[at, :, cols] = d[y * QUART : (y + 1) * QUART]
                        opay[at, :, cols] = d[(2 + y) * QUART : (3 + y) * QUART].astype(BF)
                if slots < 2:
                    o[:, cols] = ob
                    dq[:, cols] = dqb
                else:
                    o[0 : 2 * NLAT, cols] = ob[0 : 2 * NLAT]
                    dq[0 : 2 * NLAT, cols] = dqb[0 : 2 * NLAT]
                for z in range(slots):
                    ox, dqx, dk, dv, gx = done.pop(0)
                    if slots == 1:
                        xo[0, :, cols] = ox
                        xo[1, :, cols] = dqx
                    else:
                        rows = slice((2 + z) * NLAT, (3 + z) * NLAT)
                        o[rows, cols] = ob[rows] + ox
                        dq[rows, cols] = dqb[rows] + dqx
                    for h in range(2):
                        rows = slice(h * 2 * QUART, (h + 1) * 2 * QUART)
                        grads[2 * z + h][:, wk] = dk[rows].astype(BF)
                        grads[2 * z + h][:, wv] = dv[rows].astype(BF)
                    gs = gs + gx
                gacc[pl.ds(c * GRP + n, 1), :] = gs

    @pl.when(source >= 0)
    def _():
        work(1)

    @pl.when(hot)
    def _():
        work(2)

    @pl.when((source < 0) & jnp.logical_not(hot))
    def _():
        work(0)

    @pl.when(c == pl.num_programs(0) - 1)
    def _():
        gate[...] = jnp.sum(gacc[...].T, axis=0, keepdims=True)


def pair_kernel(pay, got, gate, dst):
    for d in range(16):
        dst[d, :, 0:COLS] = (pay[d] + got[d].astype(F32)).astype(BF)
    val = split3(gate[...])
    for d in range(16):
        dst[d, :, COLS:WIDE] = val


def collect_kernel(got, dst, gate):
    total = got[0].astype(F32)
    for p in range(1, 16):
        total += got[p].astype(F32)
    gate[...] = jnp.sum(total[:, COLS:WIDE], axis=0, keepdims=True)
    val = total[:, 0:COLS].astype(BF)
    for j in range(8):
        dst[j] = val


def sort_kernel(here, r0, r1, r2, r3, own, give):
    chip = here[0] // 2
    step = jnp.where(chip // 4 % 2 == 0, chip % 2, chip % 4)
    for s, r in enumerate((r0, r1, r2, r3)):

        @pl.when(step == s)
        def _():
            own[...] = r[0:QUART]
            give[...] = r[QUART : 2 * QUART]


def assemble_kernel(here, images, partner, got, own, given, dst):
    ctx, lead = place(here, images, partner)
    image = ctx // 4
    low = (image > 3) & (image < 6) | (image < lead)
    held = low == (ctx % 2 == 0)

    @pl.when(image == lead)
    def _():
        for i in range(8):
            dst[:, i * COLS : (i + 1) * COLS] = got[i]

    @pl.when((image != lead) & held)
    def _():
        dst[...] = own[...]

    @pl.when((image != lead) & jnp.logical_not(held))
    def _():
        dst[...] = given[...]


def merge_kernel(here, images, partner, o_in, dq_in, r0, r1, o, dq, buf, sems):
    del o_in, dq_in
    ctx, lead = place(here, images, partner)

    @pl.when((ctx < 2) | (ctx >= 30))
    def _():
        for s, r in enumerate((r0, r1)):
            odd = images[step_block(ctx, s)] != lead

            @pl.when(odd)
            def _():
                pltpu.make_async_copy(r, buf.at[s], sems.at[s, 0]).start()

        for s, r in enumerate((r0, r1)):
            k = step_block(ctx, s)
            odd = images[k] != lead
            rows = pl.ds(pl.multiple_of(k * NLAT, NLAT), NLAT)

            @pl.when(odd)
            def _():
                pltpu.make_async_copy(r, buf.at[s], sems.at[s, 0]).wait()
                pltpu.make_async_copy(buf.at[s, 0], o.at[rows], sems.at[s, 1]).start()
                pltpu.make_async_copy(buf.at[s, 1], dq.at[rows], sems.at[s, 2]).start()

        for s in range(2):
            k = step_block(ctx, s)
            odd = images[k] != lead
            rows = pl.ds(pl.multiple_of(k * NLAT, NLAT), NLAT)

            @pl.when(odd)
            def _():
                pltpu.make_async_copy(buf.at[s, 0], o.at[rows], sems.at[s, 1]).wait()
                pltpu.make_async_copy(buf.at[s, 1], dq.at[rows], sems.at[s, 2]).wait()


VM = pl.BlockSpec(memory_space=pltpu.VMEM)
SM = pl.BlockSpec(memory_space=pltpu.SMEM)
HBM = pl.BlockSpec(memory_space=pltpu.HBM)
ANY = pl.BlockSpec(memory_space=pl.ANY)
LIMIT = 48 * 1024 * 1024


def shape(*dims, dtype=BF):
    return jax.ShapeDtypeStruct(dims, dtype)


def call(kernel, name, out_shape, in_specs, out_specs, cost=(0, 0), **more):
    estimate = pl.CostEstimate(flops=cost[0], bytes_accessed=cost[1], transcendentals=0)
    params = pltpu.CompilerParams(vmem_limit_bytes=LIMIT)
    return pl.pallas_call(
        kernel,
        name=name,
        out_shape=out_shape,
        in_specs=in_specs,
        out_specs=out_specs,
        compiler_params=params,
        cost_estimate=estimate,
        **more,
    )


def over_dp(x):
    for far in (1, 2, 4):
        x = x + lax.ppermute(x, "dp", [(s, s ^ far) for s in range(8)])
    return x


def body(queries, latent_kv, media, gate, grad_out):
    q, g, kv_rows = queries[0], grad_out[0], latent_kv[0]
    tokens, width = q.shape
    here = lax.axis_index(CTX).astype(jnp.int32)[None]
    images = media[0]
    partner = lax.ppermute(images, "c", [(0, 1), (1, 0)])
    where = (here, images, partner)

    packed = call(
        pack_kernel,
        "pack",
        [shape(2, NLAT, width)] * 2,
        [SM, HBM, HBM],
        [HBM] * 2,
        scratch_shapes=[
            pltpu.VMEM((2, 2, NLAT, width), BF),
            pltpu.SemaphoreType.DMA((2, 2, 2)),
        ],
    )(here, q, g)
    after = packed[:1] if DEP_CHUNK else []
    chunks = call(
        chunk_kernel,
        "chunk",
        shape(8, QUART, COLS),
        [HBM] * (1 + len(after)),
        VM,
        scratch_shapes=[pltpu.SemaphoreType.DMA((8,))],
    )(kv_rows, *after)
    mixed = lax.all_to_all(chunks, IMG, 0, 0, tiled=True)
    sent = [lax.ppermute(packed[s], CTX, BLOCK_PAIRS[s]) for s in range(2)]
    chip_rows = call(half_kernel, "half", shape(2 * QUART, 2 * width), [VM, VM], VM)(
        kv_rows, lax.ppermute(kv_rows, "c", [(0, 1), (1, 0)])
    )
    lent = [lax.ppermute(chip_rows, CTX, latent_pairs(s)) for s in range(4)]

    after = sent[:DEP_SPREAD] + lent[:DEP_LENT]
    spread = call(
        spread_kernel, "spread", shape(16, QUART, COLS), [SM, SM, SM, VM, *[HBM] * len(after)], VM
    )(*where, mixed, *after)
    mine = lax.all_to_all(spread, CHIP, 0, 0, tiled=True).reshape(2, 4, 2, QUART, COLS)
    other = lax.ppermute(mine, "c", [(0, 1), (1, 0)])

    tanh_gate = jnp.tanh(gate)
    wide = pl.BlockSpec((tokens, COLS), lambda c: (0, c))
    half = pl.BlockSpec((2, 1, 2, QUART, COLS), lambda c: (0, c, 0, 0, 0))
    o, dq, xo, pay, opay, y0, y1, y2, y3, gpart = call(
        attention_kernel,
        "attention",
        [
            shape(tokens, width),
            shape(tokens, width),
            shape(2, NLAT, width),
            shape(16, QUART, COLS, dtype=F32),
            shape(16, QUART, COLS),
            *[shape(2 * QUART, 2 * width)] * 4,
            shape(1, HS, dtype=F32),
        ],
        [SM, SM, SM, SM, wide, wide, half, half, *[VM] * 4, *[HBM] * 2],
        [wide, wide, pl.BlockSpec((2, NLAT, COLS), lambda c: (0, 0, c)), *[VM] * 7],
        grid=(4,),
        scratch_shapes=[
            pltpu.VMEM((2, NLAT, width), BF),
            pltpu.VMEM((HS, HS), F32),
            pltpu.SemaphoreType.DMA,
        ],
    )(*where, tanh_gate, q, g, mine, other, *lent, *sent)

    gsum = gpart + lax.ppermute(gpart, "c", [(0, 1), (1, 0)])
    if GATE_FIRST:
        gsum = over_dp(gsum)
    theirs = lax.ppermute(opay, "c", [(0, 1), (1, 0)])
    paired = call(pair_kernel, "pair", shape(16, QUART, WIDE), [VM, VM, VM], VM)(
        pay, theirs, gsum
    )
    parts = lax.all_to_all(paired, CHIP, 0, 0, tiled=True)
    owned = [
        lax.ppermute(y, CTX, back(latent_pairs(s))) for s, y in enumerate((y0, y1, y2, y3))
    ]
    own, give = call(
        sort_kernel, "sort", [shape(QUART, 2 * width)] * 2, [SM, *[VM] * 4], [VM, VM]
    )(here, *owned)
    given = lax.ppermute(give, "c", [(0, 1), (1, 0)])
    ready = [lax.ppermute(xo, CTX, back(BLOCK_PAIRS[s])) for s in range(2)]
    summed, gates = call(
        collect_kernel,
        "collect",
        [shape(8, QUART, COLS), shape(1, HS, dtype=F32)],
        [VM],
        [VM, VM],
    )(parts)
    if not GATE_FIRST:
        gates = over_dp(gates)
    final = lax.all_to_all(summed, IMG, 0, 0, tiled=True)
    latent_grad = call(
        assemble_kernel, "assemble", shape(QUART, 2 * width), [SM, SM, SM, VM, VM, VM], VM
    )(*where, final, own, given)
    o, dq = call(
        merge_kernel,
        "merge",
        [shape(tokens, width)] * 2,
        [SM, SM, SM, *[ANY] * 4],
        [ANY, ANY],
        scratch_shapes=[
            pltpu.VMEM((2, 2, NLAT, width), BF),
            pltpu.SemaphoreType.DMA((2, 3)),
        ],
        input_output_aliases={3: 0, 4: 1},
    )(*where, o, dq, *ready)
    gate_grad = (1.0 - tanh_gate * tanh_gate) * gates[0, :HEADS]
    return o[None], dq[None], latent_grad[None], gate_grad


def solution(mesh):
    fine = Mesh(mesh.devices.reshape(8, 4, 2, 2, 2), ("dp", "x", "yh", "yl", "c"))
    wide = P("dp", CTX, None)
    return jax.shard_map(
        body,
        mesh=fine,
        in_specs=(wide, wide, P("dp", CTX), P(), wide),
        out_specs=(wide, wide, wide, P()),
        check_vma=False,
    )
```

```python
import jax
import jax.numpy as jnp
from jax import lax
from jax.experimental import pallas as pl
from jax.experimental.pallas import tpu as pltpu
from jax.sharding import Mesh
from jax.sharding import PartitionSpec as P

CTX = ("x", "yh", "yl", "c")
CHIP = ("x", "yh", "yl")
IMG = ("x", "yh")
NLAT = 64
HEADS = 32
HS = 128
GRP = 8
BATCH = 4
COLS = GRP * HS
WIDE = COLS + 128
QUART = 16
SCALE = HS**-0.5
BF = jnp.bfloat16
F32 = jnp.float32

BLOCK_PAIRS = (
    [(0, 2), (1, 7), (31, 25)],
    [(0, 8), (1, 25), (30, 22), (31, 7)],
)
WORK = (
    (2, 0, True, 0),
    (8, 1, True, 1),
    (22, 1, False, 1),
    (7, 4, True, 0),
    (7, 4, False, 1),
    (25, 5, True, 1),
    (25, 5, False, 0),
)


def latent_pairs(s):
    s = (s + 2) % 4
    pairs = [(2 * (4 + s), 0), (2 * (4 + s) + 1, 30), (2 * (12 + s) + 1, 31)]
    if s < 2:
        pairs.append((2 * (12 + s), 1))
        pairs += [(2 * s, 2), (2 * (2 + s), 8), (2 * (2 + s) + 1, 22)]
        pairs += [(2 * (8 + s), 7), (2 * (10 + s), 25)]
    return pairs


def back(pairs):
    return [(b, a) for a, b in pairs]


def nt(a, b):
    return lax.dot_general(a, b, (((1,), (1,)), ((), ())), preferred_element_type=F32)


def tn(a, b):
    return lax.dot_general(a, b, (((0,), (0,)), ((), ())), preferred_element_type=F32)


def nn(a, b):
    return lax.dot_general(a, b, (((1,), (0,)), ((), ())), preferred_element_type=F32)


def pick(cases, default):
    out = jnp.int32(default)
    for cond, value in cases:
        out = jnp.where(cond, jnp.int32(value), out)
    return out


def step_block(ctx, s):
    return jnp.where(ctx == 31, jnp.int32(1 - s), jnp.int32(s))


def sends(ctx, s):
    return (ctx < 2) | (ctx == 31) | ((ctx == 30) & (s == 1))


def chunk_kernel(images, src, dst, sems):
    copies = [
        pltpu.make_async_copy(
            src.at[:, pl.ds(i * COLS, COLS)], dst.at[i, :, pl.ds(0, COLS)], sems.at[i]
        )
        for i in range(8)
    ]
    for copy in copies:
        copy.start()
    known = jnp.full((QUART, WIDE - COLS), images[0].astype(F32)).astype(BF)
    for i in range(8):
        dst[i, :, COLS:WIDE] = known
    for copy in copies:
        copy.wait()


def pack_kernel(here, q, g, d0, d1, buf, sems):
    ctx = here[0]

    def loads(s):
        rows = pl.ds(pl.multiple_of(step_block(ctx, s) * NLAT, NLAT), NLAT)
        return [
            pltpu.make_async_copy(ref.at[rows], buf.at[s, a], sems.at[0, s, a])
            for a, ref in enumerate((q, g))
        ]

    def stores(s):
        d = (d0, d1)[s]
        return [
            pltpu.make_async_copy(buf.at[s, a], d.at[a], sems.at[1, s, a]) for a in range(2)
        ]

    for s in range(2):

        @pl.when(sends(ctx, s))
        def _():
            for copy in loads(s):
                copy.start()

    for s in range(2):

        @pl.when(sends(ctx, s))
        def _():
            for load, store in zip(loads(s), stores(s)):
                load.wait()
                store.start()

    for s in range(2):

        @pl.when(sends(ctx, s))
        def _():
            for copy in stores(s):
                copy.wait()


def half_kernel(own, other, dst):
    dst[0:QUART] = own[...]
    dst[QUART : 2 * QUART] = other[...]


def spread_kernel(got, dst, lead):
    first = jnp.max(got[3, :, COLS:WIDE].astype(F32)).astype(jnp.int32)
    lead[0] = first
    sel = got[first, :, 0:COLS]
    for p in range(16):
        dst[p] = sel


def heads_side_by_side(items):
    s = [nt(k, q) for q, g, k, v, t, keep in items]
    gf = [g.astype(F32) for q, g, k, v, t, keep in items]
    dm = [(it[4] * f).astype(BF) for it, f in zip(items, gf)]
    dp = [nt(it[3], d) for it, d in zip(items, dm)]
    e = [jnp.exp((x - jnp.max(x, axis=0, keepdims=True)) * SCALE) for x in s]
    p = [x * (it[5] / jnp.sum(x, axis=0, keepdims=True)) for it, x in zip(items, e)]
    pb = [x.astype(BF) for x in p]
    mix = [tn(x, it[3]) for it, x in zip(items, pb)]
    inner = [jnp.sum(a * b, axis=0, keepdims=True) for a, b in zip(p, dp)]
    ds = [(a * (b - c)).astype(BF) for a, b, c in zip(p, dp, inner)]
    dv = [nn(a, b) for a, b in zip(pb, dm)]
    dq = [tn(a, it[2]) * SCALE for it, a in zip(items, ds)]
    dk = [nn(a, it[0]) * SCALE for it, a in zip(items, ds)]
    gs = [jnp.sum(a * b, axis=0, keepdims=True) for a, b in zip(gf, mix)]
    out = [(it[4] * m).astype(BF) for it, m in zip(items, mix)]
    return list(zip(out, [x.astype(BF) for x in dq], dk, dv, gs))


def split3(x):
    hi = x.astype(BF).astype(F32)
    mid = (x - hi).astype(BF).astype(F32)
    lo = x - hi - mid
    row = lax.broadcasted_iota(jnp.int32, (16, x.shape[1]), 0)
    val = jnp.where(row == 0, hi, jnp.where(row == 1, mid, jnp.where(row == 2, lo, 0.0)))
    return val.astype(BF)


def attention_kernel(
    here, images, lead_ref, tg, q, g, mine, other, l0, l1, l2, l3, x0, x1,
    o, dq, xo, pay, opay, y0, y1, y2, y3, gate, xbuf, gacc, sem,
):
    c = pl.program_id(0)
    tokens = q.shape[0]
    width = o.shape[1] * 4
    ctx, lead = here[0], lead_ref[0]
    latents = (l2, l3, l0, l1)
    grads = (y2, y3, y0, y1)
    source = pick(
        [((ctx == w) & ((lead > j) if low else (lead < j)), s) for w, j, low, s in WORK], -1
    )
    hot = (ctx < 2) | (ctx >= 30)

    @pl.when(c == 0)
    def _():
        gacc[...] = jnp.zeros_like(gacc)
        for n, x in enumerate((x0, x1)):

            @pl.when(source == n)
            def _():
                copy = pltpu.make_async_copy(x, xbuf, sem)
                copy.start()
                copy.wait()

    block = lax.broadcasted_iota(jnp.int32, (1, tokens), 1) // (tokens // 4)
    keep = jnp.zeros((1, tokens), F32)
    for b in range(4):
        keep = jnp.where((block == b) & (images[b] == lead), 1.0, keep)
    ones = jnp.ones((1, NLAT), F32)
    stays = [jnp.where(images[k] == lead, 0.0, ones) for k in (2, 3)]

    def work(slots):
        for first in range(0, GRP, BATCH):
            items, heads = [], range(first, first + BATCH)
            for n in heads:
                cols = slice(n * HS, n * HS + HS)
                t = tg[c * GRP + n]
                k = [ref[0, 0, y, :, cols] for ref in (mine, other) for y in range(2)]
                v = [ref[1, 0, y, :, cols] for ref in (mine, other) for y in range(2)]
                k, v = jnp.concatenate(k, axis=0), jnp.concatenate(v, axis=0)
                items.append((q[:, cols], g[:, cols], k, v, t, keep))
                wk = pl.ds(pl.multiple_of(c * COLS + n * HS, HS), HS)
                wv = pl.ds(pl.multiple_of(width + c * COLS + n * HS, HS), HS)
                for z in range(slots):
                    k = jnp.concatenate([ref[:, wk] for ref in latents[2 * z : 2 * z + 2]], axis=0)
                    v = jnp.concatenate([ref[:, wv] for ref in latents[2 * z : 2 * z + 2]], axis=0)
                    if slots == 1:
                        items.append((xbuf[0, :, wk], xbuf[1, :, wk], k, v, t, ones))
                    else:
                        rows = slice((2 + z) * NLAT, (3 + z) * NLAT)
                        items.append((q[rows, cols], g[rows, cols], k, v, t, stays[z]))
            done = heads_side_by_side(items)
            for n in heads:
                cols = slice(n * HS, n * HS + HS)
                wk = pl.ds(pl.multiple_of(c * COLS + n * HS, HS), HS)
                wv = pl.ds(pl.multiple_of(width + c * COLS + n * HS, HS), HS)
                ob, dqb, dk, dv, gs = done.pop(0)
                for kv, d in enumerate((dk, dv)):
                    for y in range(2):
                        at = kv * 8 + c * 2 + y
                        pay[at, :, cols] = d[y * QUART : (y + 1) * QUART]
                        opay[at, :, cols] = d[(2 + y) * QUART : (3 + y) * QUART].astype(BF)
                if slots < 2:
                    o[:, cols] = ob
                    dq[:, cols] = dqb
                else:
                    o[0 : 2 * NLAT, cols] = ob[0 : 2 * NLAT]
                    dq[0 : 2 * NLAT, cols] = dqb[0 : 2 * NLAT]
                for z in range(slots):
                    ox, dqx, dk, dv, gx = done.pop(0)
                    if slots == 1:
                        xo[0, :, cols] = ox
                        xo[1, :, cols] = dqx
                    else:
                        rows = slice((2 + z) * NLAT, (3 + z) * NLAT)
                        o[rows, cols] = ob[rows] + ox
                        dq[rows, cols] = dqb[rows] + dqx
                    for h in range(2):
                        rows = slice(h * 2 * QUART, (h + 1) * 2 * QUART)
                        grads[2 * z + h][:, wk] = dk[rows].astype(BF)
                        grads[2 * z + h][:, wv] = dv[rows].astype(BF)
                    gs = gs + gx
                gacc[pl.ds(c * GRP + n, 1), :] = gs

    @pl.when(source >= 0)
    def _():
        work(1)

    @pl.when(hot)
    def _():
        work(2)

    @pl.when((source < 0) & jnp.logical_not(hot))
    def _():
        work(0)

    @pl.when(c == pl.num_programs(0) - 1)
    def _():
        gs = jnp.sum(gacc[...].T, axis=0, keepdims=True)
        gate[...] = gs
        opay[16] = jnp.zeros((QUART, COLS), BF)
        opay[16, :, 0:HS] = split3(gs)


def pair_kernel(pay, got, gate, dst):
    for d in range(16):
        dst[d, :, 0:COLS] = (pay[d] + got[d].astype(F32)).astype(BF)
    other = jnp.sum(got[16, :, 0:HS].astype(F32), axis=0, keepdims=True)
    gates = split3(gate[...] + other)
    for d in range(16):
        dst[d, :, COLS:WIDE] = gates


def collect_kernel(got, dst, gate):
    total = got[0].astype(F32)
    for p in range(1, 16):
        total += got[p].astype(F32)
    gate[...] = jnp.sum(total[:, COLS:WIDE], axis=0, keepdims=True)
    val = total[:, 0:COLS].astype(BF)
    for j in range(8):
        dst[j] = val


def sort_kernel(here, r0, r1, r2, r3, own, give):
    chip = here[0] // 2
    step = jnp.where(chip // 4 % 2 == 0, chip % 2, chip % 4)
    for s, r in enumerate((r2, r3, r0, r1)):

        @pl.when(step == s)
        def _():
            own[...] = r[0:QUART]
            give[...] = r[QUART : 2 * QUART]


def assemble_kernel(here, lead_ref, got, own, given, dst):
    ctx, lead = here[0], lead_ref[0]
    image = ctx // 4
    low = (image > 3) & (image < 6) | (image < lead)
    held = low == (ctx % 2 == 0)

    @pl.when(image == lead)
    def _():
        for i in range(8):
            dst[:, i * COLS : (i + 1) * COLS] = got[i]

    @pl.when((image != lead) & held)
    def _():
        dst[...] = own[...]

    @pl.when((image != lead) & jnp.logical_not(held))
    def _():
        dst[...] = given[...]


def merge_kernel(here, images, lead_ref, o_in, dq_in, r0, r1, o, dq, buf, sems):
    del o_in, dq_in
    ctx, lead = here[0], lead_ref[0]

    def odd(s):
        return sends(ctx, s) & (images[step_block(ctx, s)] != lead)

    def load(s):
        return pltpu.make_async_copy((r0, r1)[s], buf.at[s], sems.at[s, 0])

    def stores(s):
        rows = pl.ds(pl.multiple_of(step_block(ctx, s) * NLAT, NLAT), NLAT)
        return (
            pltpu.make_async_copy(buf.at[s, 0], o.at[rows], sems.at[s, 1]),
            pltpu.make_async_copy(buf.at[s, 1], dq.at[rows], sems.at[s, 2]),
        )

    for s in range(2):

        @pl.when(odd(s))
        def _():
            load(s).start()

    for s in range(2):

        @pl.when(odd(s))
        def _():
            load(s).wait()
            for copy in stores(s):
                copy.start()

    for s in range(2):

        @pl.when(odd(s))
        def _():
            for copy in stores(s):
                copy.wait()


VM = pl.BlockSpec(memory_space=pltpu.VMEM)
SM = pl.BlockSpec(memory_space=pltpu.SMEM)
HBM = pl.BlockSpec(memory_space=pltpu.HBM)
ANY = pl.BlockSpec(memory_space=pl.ANY)
LIMIT = 48 * 1024 * 1024


def shape(*dims, dtype=BF):
    return jax.ShapeDtypeStruct(dims, dtype)


def call(kernel, name, out_shape, in_specs, out_specs, cost=(0, 0), **more):
    estimate = pl.CostEstimate(flops=cost[0], bytes_accessed=cost[1], transcendentals=0)
    params = pltpu.CompilerParams(vmem_limit_bytes=LIMIT)
    return pl.pallas_call(
        kernel,
        name=name,
        out_shape=out_shape,
        in_specs=in_specs,
        out_specs=out_specs,
        compiler_params=params,
        cost_estimate=estimate,
        **more,
    )


def body(queries, latent_kv, media, gate, grad_out):
    q, g, kv_rows = queries[0], grad_out[0], latent_kv[0]
    tokens, width = q.shape
    here = lax.axis_index(CTX).astype(jnp.int32)[None]
    images = media[0]
    swap = [(0, 1), (1, 0)]

    packed = call(
        pack_kernel,
        "pack",
        [shape(2, NLAT, width)] * 2,
        [SM, HBM, HBM],
        [HBM] * 2,
        scratch_shapes=[
            pltpu.VMEM((2, 2, NLAT, width), BF),
            pltpu.SemaphoreType.DMA((2, 2, 2)),
        ],
    )(here, q, g)
    chunks = call(
        chunk_kernel,
        "chunk",
        shape(8, QUART, WIDE),
        [SM, HBM],
        VM,
        scratch_shapes=[pltpu.SemaphoreType.DMA((8,))],
    )(images, kv_rows)
    mixed = lax.all_to_all(chunks, IMG, 0, 0, tiled=True)
    sent = [lax.ppermute(packed[s], CTX, BLOCK_PAIRS[s]) for s in range(2)]
    chip_rows = call(half_kernel, "half", shape(2 * QUART, 2 * width), [VM, VM], VM)(
        kv_rows, lax.ppermute(kv_rows, "c", swap)
    )
    lent = [lax.ppermute(chip_rows, CTX, latent_pairs(s)) for s in range(4)]

    spread, lead = call(
        spread_kernel,
        "spread",
        [shape(16, QUART, COLS), shape(1, dtype=jnp.int32)],
        [VM],
        [VM, SM],
    )(mixed)
    mine = lax.all_to_all(spread, CHIP, 0, 0, tiled=True).reshape(2, 4, 2, QUART, COLS)
    other = lax.ppermute(mine, "c", swap)

    tanh_gate = jnp.tanh(gate)
    wide = pl.BlockSpec((tokens, COLS), lambda c: (0, c))
    half = pl.BlockSpec((2, 1, 2, QUART, COLS), lambda c: (0, c, 0, 0, 0))
    o, dq, xo, pay, opay, y0, y1, y2, y3, gpart = call(
        attention_kernel,
        "attention",
        [
            shape(tokens, width),
            shape(tokens, width),
            shape(2, NLAT, width),
            shape(16, QUART, COLS, dtype=F32),
            shape(17, QUART, COLS),
            *[shape(2 * QUART, 2 * width)] * 4,
            shape(1, HS, dtype=F32),
        ],
        [SM, SM, SM, SM, wide, wide, half, half, *[VM] * 4, HBM, HBM],
        [wide, wide, pl.BlockSpec((2, NLAT, COLS), lambda c: (0, 0, c)), *[VM] * 7],
        grid=(4,),
        scratch_shapes=[
            pltpu.VMEM((2, NLAT, width), BF),
            pltpu.VMEM((HS, HS), F32),
            pltpu.SemaphoreType.DMA,
        ],
    )(here, images, lead, tanh_gate, q, g, mine, other, *lent, *sent)

    theirs = lax.ppermute(opay, "c", swap)
    paired = call(pair_kernel, "pair", shape(16, QUART, WIDE), [VM, VM, VM], VM)(
        pay, theirs, gpart
    )
    parts = lax.all_to_all(paired, CHIP, 0, 0, tiled=True)
    owned = [lax.ppermute(y, CTX, back(latent_pairs(s))) for s, y in enumerate((y0, y1, y2, y3))]
    own, give = call(
        sort_kernel, "sort", [shape(QUART, 2 * width)] * 2, [SM, *[VM] * 4], [VM, VM]
    )(here, *owned)
    given = lax.ppermute(give, "c", swap)
    ready = [lax.ppermute(xo, CTX, back(BLOCK_PAIRS[s])) for s in range(2)]
    summed, gates = call(
        collect_kernel,
        "collect",
        [shape(8, QUART, COLS), shape(1, HS, dtype=F32)],
        [VM],
        [VM, VM],
    )(parts)
    for flip in (1, 2, 7):
        gates = gates + lax.ppermute(gates, "dp", [(s, s ^ flip) for s in range(8)])
    final = lax.all_to_all(summed, IMG, 0, 0, tiled=True)
    latent_grad = call(
        assemble_kernel, "assemble", shape(QUART, 2 * width), [SM, SM, VM, VM, VM], VM
    )(here, lead, final, own, given)
    o, dq = call(
        merge_kernel,
        "merge",
        [shape(tokens, width)] * 2,
        [SM, SM, SM, *[ANY] * 4],
        [ANY, ANY],
        scratch_shapes=[
            pltpu.VMEM((2, 2, NLAT, width), BF),
            pltpu.SemaphoreType.DMA((2, 3)),
        ],
        input_output_aliases={3: 0, 4: 1},
    )(here, images, lead, o, dq, *ready)
    gate_grad = (1.0 - tanh_gate * tanh_gate) * gates[0, :HEADS]
    return o[None], dq[None], latent_grad[None], gate_grad


def solution(mesh):
    fine = Mesh(mesh.devices.reshape(8, 4, 2, 2, 2), ("dp", "x", "yh", "yl", "c"))
    wide = P("dp", CTX, None)
    return jax.shard_map(
        body,
        mesh=fine,
        in_specs=(wide, wide, P("dp", CTX), P(), wide),
        out_specs=(wide, wide, wide, P()),
        check_vma=False,
    )
```

```python
import jax
import jax.numpy as jnp
from jax import lax
from jax.experimental import pallas as pl
from jax.experimental.pallas import tpu as pltpu
from jax.sharding import Mesh
from jax.sharding import PartitionSpec as P

CTX = ("x", "yh", "yl", "c")
CHIP = ("x", "yh", "yl")
IMG = ("x", "yh")
NLAT = 64
HEADS = 32
HS = 128
GRP = 8
BATCH = 4
COLS = GRP * HS
WIDE = COLS + 128
QUART = 16
SCALE = HS**-0.5
BF = jnp.bfloat16
F32 = jnp.float32

BLOCK_PAIRS = (
    [(0, 2), (1, 7), (31, 25)],
    [(0, 8), (1, 25), (30, 22), (31, 7)],
)
WORK = (
    (2, 0, True, 0),
    (8, 1, True, 1),
    (22, 1, False, 1),
    (7, 4, True, 0),
    (7, 4, False, 1),
    (25, 5, True, 1),
    (25, 5, False, 0),
)


def latent_pairs(s):
    s = (s + 2) % 4
    pairs = [(2 * (4 + s), 0), (2 * (4 + s) + 1, 30), (2 * (12 + s) + 1, 31)]
    if s < 2:
        pairs.append((2 * (12 + s), 1))
        pairs += [(2 * s, 2), (2 * (2 + s), 8), (2 * (2 + s) + 1, 22)]
        pairs += [(2 * (8 + s), 7), (2 * (10 + s), 25)]
    return pairs


def back(pairs):
    return [(b, a) for a, b in pairs]


def nt(a, b):
    return lax.dot_general(a, b, (((1,), (1,)), ((), ())), preferred_element_type=F32)


def tn(a, b):
    return lax.dot_general(a, b, (((0,), (0,)), ((), ())), preferred_element_type=F32)


def nn(a, b):
    return lax.dot_general(a, b, (((1,), (0,)), ((), ())), preferred_element_type=F32)


def pick(cases, default):
    out = jnp.int32(default)
    for cond, value in cases:
        out = jnp.where(cond, jnp.int32(value), out)
    return out


def step_block(ctx, s):
    return jnp.where(ctx == 31, jnp.int32(1 - s), jnp.int32(s))


def sends(ctx, s):
    return (ctx < 2) | (ctx == 31) | ((ctx == 30) & (s == 1))


def chunk_kernel(images, src, dst):
    known = jnp.full((QUART, WIDE - COLS), images[0].astype(F32)).astype(BF)
    for i in range(8):
        dst[i, :, 0:COLS] = src[:, i * COLS : (i + 1) * COLS]
        dst[i, :, COLS:WIDE] = known


def pack_kernel(here, q, g, d0, d1, buf, sems):
    ctx = here[0]

    def loads(s):
        rows = pl.ds(pl.multiple_of(step_block(ctx, s) * NLAT, NLAT), NLAT)
        return [
            pltpu.make_async_copy(ref.at[rows], buf.at[s, a], sems.at[0, s, a])
            for a, ref in enumerate((q, g))
        ]

    def stores(s):
        d = (d0, d1)[s]
        return [
            pltpu.make_async_copy(buf.at[s, a], d.at[a], sems.at[1, s, a]) for a in range(2)
        ]

    for s in range(2):

        @pl.when(sends(ctx, s))
        def _():
            for copy in loads(s):
                copy.start()

    for s in range(2):

        @pl.when(sends(ctx, s))
        def _():
            for load, store in zip(loads(s), stores(s)):
                load.wait()
                store.start()

    for s in range(2):

        @pl.when(sends(ctx, s))
        def _():
            for copy in stores(s):
                copy.wait()


def half_kernel(own, other, dst):
    dst[0:QUART] = own[...]
    dst[QUART : 2 * QUART] = other[...]


def spread_kernel(got, dst, lead):
    first = jnp.max(got[3, :, COLS:WIDE].astype(F32)).astype(jnp.int32)
    lead[0] = first
    sel = got[first, :, 0:COLS]
    for p in range(16):
        dst[p] = sel


def heads_side_by_side(items):
    s = [nt(k, q) for q, g, k, v, t, keep in items]
    gf = [g.astype(F32) for q, g, k, v, t, keep in items]
    dm = [(it[4] * f).astype(BF) for it, f in zip(items, gf)]
    dp = [nt(it[3], d) for it, d in zip(items, dm)]
    e = [jnp.exp((x - jnp.max(x, axis=0, keepdims=True)) * SCALE) for x in s]
    p = [x * (it[5] / jnp.sum(x, axis=0, keepdims=True)) for it, x in zip(items, e)]
    pb = [x.astype(BF) for x in p]
    mix = [tn(x, it[3]) for it, x in zip(items, pb)]
    inner = [jnp.sum(a * b, axis=0, keepdims=True) for a, b in zip(p, dp)]
    ds = [(a * (b - c)).astype(BF) for a, b, c in zip(p, dp, inner)]
    dv = [nn(a, b) for a, b in zip(pb, dm)]
    dq = [tn(a, it[2]) * SCALE for it, a in zip(items, ds)]
    dk = [nn(a, it[0]) * SCALE for it, a in zip(items, ds)]
    gs = [jnp.sum(a * b, axis=0, keepdims=True) for a, b in zip(gf, mix)]
    out = [(it[4] * m).astype(BF) for it, m in zip(items, mix)]
    return list(zip(out, [x.astype(BF) for x in dq], dk, dv, gs))


def split3(x):
    hi = x.astype(BF).astype(F32)
    mid = (x - hi).astype(BF).astype(F32)
    lo = x - hi - mid
    row = lax.broadcasted_iota(jnp.int32, (16, x.shape[1]), 0)
    val = jnp.where(row == 0, hi, jnp.where(row == 1, mid, jnp.where(row == 2, lo, 0.0)))
    return val.astype(BF)


def attention_kernel(
    here, images, lead_ref, tg, q, g, mine, other, l0, l1, l2, l3, x0, x1,
    o, dq, xo, pay, opay, y0, y1, y2, y3, gate, xbuf, gacc, sem,
):
    c = pl.program_id(0)
    tokens = q.shape[0]
    width = o.shape[1] * 4
    ctx, lead = here[0], lead_ref[0]
    latents = (l2, l3, l0, l1)
    grads = (y2, y3, y0, y1)
    source = pick(
        [((ctx == w) & ((lead > j) if low else (lead < j)), s) for w, j, low, s in WORK], -1
    )
    hot = (ctx < 2) | (ctx >= 30)

    @pl.when(c == 0)
    def _():
        gacc[...] = jnp.zeros_like(gacc)
        for n, x in enumerate((x0, x1)):

            @pl.when(source == n)
            def _():
                copy = pltpu.make_async_copy(x, xbuf, sem)
                copy.start()
                copy.wait()

    block = lax.broadcasted_iota(jnp.int32, (1, tokens), 1) // (tokens // 4)
    keep = jnp.zeros((1, tokens), F32)
    for b in range(4):
        keep = jnp.where((block == b) & (images[b] == lead), 1.0, keep)
    ones = jnp.ones((1, NLAT), F32)
    stays = [jnp.where(images[k] == lead, 0.0, ones) for k in (2, 3)]

    def work(slots):
        for first in range(0, GRP, BATCH):
            items, heads = [], range(first, first + BATCH)
            for n in heads:
                cols = slice(n * HS, n * HS + HS)
                t = tg[c * GRP + n]
                k = [ref[0, 0, y, :, cols] for ref in (mine, other) for y in range(2)]
                v = [ref[1, 0, y, :, cols] for ref in (mine, other) for y in range(2)]
                k, v = jnp.concatenate(k, axis=0), jnp.concatenate(v, axis=0)
                items.append((q[:, cols], g[:, cols], k, v, t, keep))
                wk = pl.ds(pl.multiple_of(c * COLS + n * HS, HS), HS)
                wv = pl.ds(pl.multiple_of(width + c * COLS + n * HS, HS), HS)
                for z in range(slots):
                    k = jnp.concatenate([ref[:, wk] for ref in latents[2 * z : 2 * z + 2]], axis=0)
                    v = jnp.concatenate([ref[:, wv] for ref in latents[2 * z : 2 * z + 2]], axis=0)
                    if slots == 1:
                        items.append((xbuf[0, :, wk], xbuf[1, :, wk], k, v, t, ones))
                    else:
                        rows = slice((2 + z) * NLAT, (3 + z) * NLAT)
                        items.append((q[rows, cols], g[rows, cols], k, v, t, stays[z]))
            done = heads_side_by_side(items)
            for n in heads:
                cols = slice(n * HS, n * HS + HS)
                wk = pl.ds(pl.multiple_of(c * COLS + n * HS, HS), HS)
                wv = pl.ds(pl.multiple_of(width + c * COLS + n * HS, HS), HS)
                ob, dqb, dk, dv, gs = done.pop(0)
                for kv, d in enumerate((dk, dv)):
                    for y in range(2):
                        at = kv * 8 + c * 2 + y
                        pay[at, :, cols] = d[y * QUART : (y + 1) * QUART]
                        opay[at, :, cols] = d[(2 + y) * QUART : (3 + y) * QUART].astype(BF)
                if slots < 2:
                    o[:, cols] = ob
                    dq[:, cols] = dqb
                else:
                    o[0 : 2 * NLAT, cols] = ob[0 : 2 * NLAT]
                    dq[0 : 2 * NLAT, cols] = dqb[0 : 2 * NLAT]
                for z in range(slots):
                    ox, dqx, dk, dv, gx = done.pop(0)
                    if slots == 1:
                        xo[0, :, cols] = ox
                        xo[1, :, cols] = dqx
                    else:
                        rows = slice((2 + z) * NLAT, (3 + z) * NLAT)
                        o[rows, cols] = ob[rows] + ox
                        dq[rows, cols] = dqb[rows] + dqx
                    for h in range(2):
                        rows = slice(h * 2 * QUART, (h + 1) * 2 * QUART)
                        grads[2 * z + h][:, wk] = dk[rows].astype(BF)
                        grads[2 * z + h][:, wv] = dv[rows].astype(BF)
                    gs = gs + gx
                gacc[pl.ds(c * GRP + n, 1), :] = gs

    @pl.when(source >= 0)
    def _():
        work(1)

    @pl.when(hot)
    def _():
        work(2)

    @pl.when((source < 0) & jnp.logical_not(hot))
    def _():
        work(0)

    @pl.when(c == pl.num_programs(0) - 1)
    def _():
        gs = jnp.sum(gacc[...].T, axis=0, keepdims=True)
        gate[...] = gs
        opay[16] = jnp.zeros((QUART, COLS), BF)
        opay[16, :, 0:HS] = split3(gs)


def pair_kernel(pay, got, gate, dst):
    for d in range(16):
        dst[d, :, 0:COLS] = (pay[d] + got[d].astype(F32)).astype(BF)
    other = jnp.sum(got[16, :, 0:HS].astype(F32), axis=0, keepdims=True)
    gates = split3(gate[...] + other)
    for d in range(16):
        dst[d, :, COLS:WIDE] = gates


def collect_kernel(got, dst, gate):
    total = got[0].astype(F32)
    for p in range(1, 16):
        total += got[p].astype(F32)
    gate[...] = jnp.sum(total[:, COLS:WIDE], axis=0, keepdims=True)
    val = total[:, 0:COLS].astype(BF)
    for j in range(8):
        dst[j] = val


def sort_kernel(here, r0, r1, r2, r3, own, give, sems):
    chip = here[0] // 2
    step = jnp.where(chip // 4 % 2 == 0, chip % 2, chip % 4)
    for s, r in enumerate((r2, r3, r0, r1)):

        @pl.when(step == s)
        def _():
            first = pltpu.make_async_copy(r.at[pl.ds(0, QUART)], own, sems.at[0])
            second = pltpu.make_async_copy(r.at[pl.ds(QUART, QUART)], give, sems.at[1])
            first.start()
            second.start()
            first.wait()
            second.wait()


def assemble_kernel(here, lead_ref, got, own, given, dst):
    ctx, lead = here[0], lead_ref[0]
    image = ctx // 4
    low = (image > 3) & (image < 6) | (image < lead)
    held = low == (ctx % 2 == 0)

    @pl.when(image == lead)
    def _():
        for i in range(8):
            dst[:, i * COLS : (i + 1) * COLS] = got[i]

    @pl.when((image != lead) & held)
    def _():
        dst[...] = own[...]

    @pl.when((image != lead) & jnp.logical_not(held))
    def _():
        dst[...] = given[...]


def merge_kernel(here, images, lead_ref, o_in, dq_in, r0, r1, o, dq, buf, sems):
    del o_in, dq_in
    ctx, lead = here[0], lead_ref[0]

    def odd(s):
        return sends(ctx, s) & (images[step_block(ctx, s)] != lead)

    def load(s):
        return pltpu.make_async_copy((r0, r1)[s], buf.at[s], sems.at[s, 0])

    def stores(s):
        rows = pl.ds(pl.multiple_of(step_block(ctx, s) * NLAT, NLAT), NLAT)
        return (
            pltpu.make_async_copy(buf.at[s, 0], o.at[rows], sems.at[s, 1]),
            pltpu.make_async_copy(buf.at[s, 1], dq.at[rows], sems.at[s, 2]),
        )

    for s in range(2):

        @pl.when(odd(s))
        def _():
            load(s).start()

    for s in range(2):

        @pl.when(odd(s))
        def _():
            load(s).wait()
            for copy in stores(s):
                copy.start()

    for s in range(2):

        @pl.when(odd(s))
        def _():
            for copy in stores(s):
                copy.wait()


VM = pl.BlockSpec(memory_space=pltpu.VMEM)
SM = pl.BlockSpec(memory_space=pltpu.SMEM)
HBM = pl.BlockSpec(memory_space=pltpu.HBM)
ANY = pl.BlockSpec(memory_space=pl.ANY)
LIMIT = 48 * 1024 * 1024
SMALL = 16 * 1024 * 1024


def shape(*dims, dtype=BF):
    return jax.ShapeDtypeStruct(dims, dtype)


def call(kernel, name, out_shape, in_specs, out_specs, cost=(0, 0), limit=SMALL, **more):
    estimate = pl.CostEstimate(flops=cost[0], bytes_accessed=cost[1], transcendentals=0)
    params = pltpu.CompilerParams(vmem_limit_bytes=limit)
    return pl.pallas_call(
        kernel,
        name=name,
        out_shape=out_shape,
        in_specs=in_specs,
        out_specs=out_specs,
        compiler_params=params,
        cost_estimate=estimate,
        **more,
    )


def body(queries, latent_kv, media, gate, grad_out):
    q, g, kv_rows = queries[0], grad_out[0], latent_kv[0]
    tokens, width = q.shape
    here = lax.axis_index(CTX).astype(jnp.int32)[None]
    images = media[0]
    swap = [(0, 1), (1, 0)]

    packed = call(
        pack_kernel,
        "pack",
        [shape(2, NLAT, width)] * 2,
        [SM, HBM, HBM],
        [HBM] * 2,
        limit=62 * 1024 * 1024,
        scratch_shapes=[
            pltpu.VMEM((2, 2, NLAT, width), BF),
            pltpu.SemaphoreType.DMA((2, 2, 2)),
        ],
    )(here, q, g)
    chunks = call(chunk_kernel, "chunk", shape(8, QUART, WIDE), [SM, VM], VM)(images, kv_rows)
    mixed = lax.all_to_all(chunks, IMG, 0, 0, tiled=True)
    sent = [lax.ppermute(packed[s], CTX, BLOCK_PAIRS[s]) for s in range(2)]
    chip_rows = call(half_kernel, "half", shape(2 * QUART, 2 * width), [VM, VM], VM)(
        kv_rows, lax.ppermute(kv_rows, "c", swap)
    )
    lent = [lax.ppermute(chip_rows, CTX, latent_pairs(s)) for s in range(4)]

    spread, lead = call(
        spread_kernel,
        "spread",
        [shape(16, QUART, COLS), shape(1, dtype=jnp.int32)],
        [VM],
        [VM, SM],
    )(mixed)
    mine = lax.all_to_all(spread, CHIP, 0, 0, tiled=True).reshape(2, 4, 2, QUART, COLS)
    other = lax.ppermute(mine, "c", swap)

    tanh_gate = jnp.tanh(gate)
    wide = pl.BlockSpec((tokens, COLS), lambda c: (0, c))
    half = pl.BlockSpec((2, 1, 2, QUART, COLS), lambda c: (0, c, 0, 0, 0))
    o, dq, xo, pay, opay, y0, y1, y2, y3, gpart = call(
        attention_kernel,
        "attention",
        [
            shape(tokens, width),
            shape(tokens, width),
            shape(2, NLAT, width),
            shape(16, QUART, COLS, dtype=F32),
            shape(17, QUART, COLS),
            *[shape(2 * QUART, 2 * width)] * 4,
            shape(1, HS, dtype=F32),
        ],
        [SM, SM, SM, SM, wide, wide, half, half, *[VM] * 4, HBM, HBM],
        [wide, wide, pl.BlockSpec((2, NLAT, COLS), lambda c: (0, 0, c)), *[VM] * 7],
        grid=(4,),
        limit=LIMIT,
        scratch_shapes=[
            pltpu.VMEM((2, NLAT, width), BF),
            pltpu.VMEM((HS, HS), F32),
            pltpu.SemaphoreType.DMA,
        ],
    )(here, images, lead, tanh_gate, q, g, mine, other, *lent, *sent)

    theirs = lax.ppermute(opay, "c", swap)
    paired = call(pair_kernel, "pair", shape(16, QUART, WIDE), [VM, VM, VM], VM)(
        pay, theirs, gpart
    )
    parts = lax.all_to_all(paired, CHIP, 0, 0, tiled=True)
    owned = [lax.ppermute(y, CTX, back(latent_pairs(s))) for s, y in enumerate((y0, y1, y2, y3))]
    own, give = call(
        sort_kernel,
        "sort",
        [shape(QUART, 2 * width)] * 2,
        [SM, *[ANY] * 4],
        [VM, VM],
        scratch_shapes=[pltpu.SemaphoreType.DMA((2,))],
    )(here, *owned)
    given = lax.ppermute(give, "c", swap)
    ready = [lax.ppermute(xo, CTX, back(BLOCK_PAIRS[s])) for s in range(2)]
    summed, gates = call(
        collect_kernel,
        "collect",
        [shape(8, QUART, COLS), shape(1, HS, dtype=F32)],
        [VM],
        [VM, VM],
    )(parts)
    for flip in (1, 2, 7):
        gates = gates + lax.ppermute(gates, "dp", [(s, s ^ flip) for s in range(8)])
    final = lax.all_to_all(summed, IMG, 0, 0, tiled=True)
    latent_grad = call(
        assemble_kernel, "assemble", shape(QUART, 2 * width), [SM, SM, VM, VM, VM], VM
    )(here, lead, final, own, given)
    o, dq = call(
        merge_kernel,
        "merge",
        [shape(tokens, width)] * 2,
        [SM, SM, SM, *[ANY] * 4],
        [ANY, ANY],
        scratch_shapes=[
            pltpu.VMEM((2, 2, NLAT, width), BF),
            pltpu.SemaphoreType.DMA((2, 3)),
        ],
        input_output_aliases={3: 0, 4: 1},
    )(here, images, lead, o, dq, *ready)
    gate_grad = (1.0 - tanh_gate * tanh_gate) * gates[0, :HEADS]
    return o[None], dq[None], latent_grad[None], gate_grad


def solution(mesh):
    fine = Mesh(mesh.devices.reshape(8, 4, 2, 2, 2), ("dp", "x", "yh", "yl", "c"))
    wide = P("dp", CTX, None)
    return jax.shard_map(
        body,
        mesh=fine,
        in_specs=(wide, wide, P("dp", CTX), P(), wide),
        out_specs=(wide, wide, wide, P()),
        check_vma=False,
    )
```

```python
import jax
import jax.numpy as jnp
from jax import lax
from jax.experimental import pallas as pl
from jax.experimental.pallas import tpu as pltpu
from jax.sharding import Mesh
from jax.sharding import PartitionSpec as P

CTX = ("x", "yh", "yl", "c")
CHIP = ("x", "yh", "yl")
IMG = ("x", "yh")
NLAT = 64
HEADS = 32
HS = 128
GRP = 8
BATCH = 4
COLS = GRP * HS
WIDE = COLS + 128
QUART = 16
SCALE = HS**-0.5
BF = jnp.bfloat16
F32 = jnp.float32

BLOCK_PAIRS = (
    [(0, 2), (1, 7), (31, 25)],
    [(0, 8), (1, 25), (30, 22), (31, 7)],
)
WORK = (
    (2, 0, True, 0),
    (8, 1, True, 1),
    (22, 1, False, 1),
    (7, 4, True, 0),
    (7, 4, False, 1),
    (25, 5, True, 1),
    (25, 5, False, 0),
)


def latent_pairs(s):
    s = (s + 2) % 4
    pairs = [(2 * (4 + s), 0), (2 * (4 + s) + 1, 30), (2 * (12 + s) + 1, 31)]
    if s < 2:
        pairs.append((2 * (12 + s), 1))
        pairs += [(2 * s, 2), (2 * (2 + s), 8), (2 * (2 + s) + 1, 22)]
        pairs += [(2 * (8 + s), 7), (2 * (10 + s), 25)]
    return pairs


def back(pairs):
    return [(b, a) for a, b in pairs]


def nt(a, b):
    return lax.dot_general(a, b, (((1,), (1,)), ((), ())), preferred_element_type=F32)


def tn(a, b):
    return lax.dot_general(a, b, (((0,), (0,)), ((), ())), preferred_element_type=F32)


def nn(a, b):
    return lax.dot_general(a, b, (((1,), (0,)), ((), ())), preferred_element_type=F32)


def pick(cases, default):
    out = jnp.int32(default)
    for cond, value in cases:
        out = jnp.where(cond, jnp.int32(value), out)
    return out


def step_block(ctx, s):
    return jnp.where(ctx == 31, jnp.int32(1 - s), jnp.int32(s))


def sends(ctx, s):
    return (ctx < 2) | (ctx == 31) | ((ctx == 30) & (s == 1))


def chunk_kernel(images, src, dst):
    known = jnp.full((QUART, WIDE - COLS), images[0].astype(F32)).astype(BF)
    for i in range(8):
        dst[i, :, 0:COLS] = src[:, i * COLS : (i + 1) * COLS]
        dst[i, :, COLS:WIDE] = known


def pack_kernel(here, q, g, d0, d1, buf, sems):
    ctx = here[0]

    def loads(s):
        rows = pl.ds(pl.multiple_of(step_block(ctx, s) * NLAT, NLAT), NLAT)
        return [
            pltpu.make_async_copy(ref.at[rows], buf.at[s, a], sems.at[0, s, a])
            for a, ref in enumerate((q, g))
        ]

    def stores(s):
        d = (d0, d1)[s]
        return [
            pltpu.make_async_copy(buf.at[s, a], d.at[a], sems.at[1, s, a]) for a in range(2)
        ]

    for s in range(2):

        @pl.when(sends(ctx, s))
        def _():
            for copy in loads(s):
                copy.start()

    for s in range(2):

        @pl.when(sends(ctx, s))
        def _():
            for load, store in zip(loads(s), stores(s)):
                load.wait()
                store.start()

    for s in range(2):

        @pl.when(sends(ctx, s))
        def _():
            for copy in stores(s):
                copy.wait()


def half_kernel(own, other, dst):
    dst[0:QUART] = own[...]
    dst[QUART : 2 * QUART] = other[...]


def spread_kernel(got, dst, lead):
    first = jnp.max(got[3, :, COLS:WIDE].astype(F32)).astype(jnp.int32)
    lead[0] = first
    sel = got[first, :, 0:COLS]
    for p in range(16):
        dst[p] = sel


def heads_side_by_side(items):
    s = [nt(k, q) for q, g, k, v, t, keep in items]
    gf = [g.astype(F32) for q, g, k, v, t, keep in items]
    dm = [(it[4] * f).astype(BF) for it, f in zip(items, gf)]
    dp = [nt(it[3], d) for it, d in zip(items, dm)]
    e = [jnp.exp((x - jnp.max(x, axis=0, keepdims=True)) * SCALE) for x in s]
    p = [x * (it[5] / jnp.sum(x, axis=0, keepdims=True)) for it, x in zip(items, e)]
    pb = [x.astype(BF) for x in p]
    mix = [tn(x, it[3]) for it, x in zip(items, pb)]
    inner = [jnp.sum(a * b, axis=0, keepdims=True) for a, b in zip(p, dp)]
    ds = [(a * (b - c)).astype(BF) for a, b, c in zip(p, dp, inner)]
    dv = [nn(a, b) for a, b in zip(pb, dm)]
    dq = [tn(a, it[2]) * SCALE for it, a in zip(items, ds)]
    dk = [nn(a, it[0]) * SCALE for it, a in zip(items, ds)]
    gs = [jnp.sum(a * b, axis=0, keepdims=True) for a, b in zip(gf, mix)]
    out = [(it[4] * m).astype(BF) for it, m in zip(items, mix)]
    return list(zip(out, [x.astype(BF) for x in dq], dk, dv, gs))


def split3(x):
    hi = x.astype(BF).astype(F32)
    mid = (x - hi).astype(BF).astype(F32)
    lo = x - hi - mid
    row = lax.broadcasted_iota(jnp.int32, (16, x.shape[1]), 0)
    val = jnp.where(row == 0, hi, jnp.where(row == 1, mid, jnp.where(row == 2, lo, 0.0)))
    return val.astype(BF)


def attention_kernel(
    here, images, lead_ref, tg, q, g, mine, other, l0, l1, l2, l3, x0, x1,
    o, dq, xo, pay, opay, y0, y1, y2, y3, gate, xbuf, gacc, sem,
):
    c = pl.program_id(0)
    tokens = q.shape[0]
    width = o.shape[1] * 4
    ctx, lead = here[0], lead_ref[0]
    latents = (l2, l3, l0, l1)
    grads = (y2, y3, y0, y1)
    source = pick(
        [((ctx == w) & ((lead > j) if low else (lead < j)), s) for w, j, low, s in WORK], -1
    )
    hot = (ctx < 2) | (ctx >= 30)

    @pl.when(c == 0)
    def _():
        gacc[...] = jnp.zeros_like(gacc)
        for n, x in enumerate((x0, x1)):

            @pl.when(source == n)
            def _():
                copy = pltpu.make_async_copy(x, xbuf, sem)
                copy.start()
                copy.wait()

    block = lax.broadcasted_iota(jnp.int32, (1, tokens), 1) // (tokens // 4)
    keep = jnp.zeros((1, tokens), F32)
    for b in range(4):
        keep = jnp.where((block == b) & (images[b] == lead), 1.0, keep)
    ones = jnp.ones((1, NLAT), F32)
    stays = [jnp.where(images[k] == lead, 0.0, ones) for k in (2, 3)]

    def work(slots):
        for first in range(0, GRP, BATCH):
            items, heads = [], range(first, first + BATCH)
            for n in heads:
                cols = slice(n * HS, n * HS + HS)
                t = tg[c * GRP + n]
                k = [ref[0, 0, y, :, cols] for ref in (mine, other) for y in range(2)]
                v = [ref[1, 0, y, :, cols] for ref in (mine, other) for y in range(2)]
                k, v = jnp.concatenate(k, axis=0), jnp.concatenate(v, axis=0)
                items.append((q[:, cols], g[:, cols], k, v, t, keep))
                wk = pl.ds(pl.multiple_of(c * COLS + n * HS, HS), HS)
                wv = pl.ds(pl.multiple_of(width + c * COLS + n * HS, HS), HS)
                for z in range(slots):
                    k = jnp.concatenate([ref[:, wk] for ref in latents[2 * z : 2 * z + 2]], axis=0)
                    v = jnp.concatenate([ref[:, wv] for ref in latents[2 * z : 2 * z + 2]], axis=0)
                    if slots == 1:
                        items.append((xbuf[0, :, wk], xbuf[1, :, wk], k, v, t, ones))
                    else:
                        rows = slice((2 + z) * NLAT, (3 + z) * NLAT)
                        items.append((q[rows, cols], g[rows, cols], k, v, t, stays[z]))
            done = heads_side_by_side(items)
            for n in heads:
                cols = slice(n * HS, n * HS + HS)
                wk = pl.ds(pl.multiple_of(c * COLS + n * HS, HS), HS)
                wv = pl.ds(pl.multiple_of(width + c * COLS + n * HS, HS), HS)
                ob, dqb, dk, dv, gs = done.pop(0)
                for kv, d in enumerate((dk, dv)):
                    for y in range(2):
                        at = kv * 8 + c * 2 + y
                        pay[at, :, cols] = d[y * QUART : (y + 1) * QUART]
                        opay[at, :, cols] = d[(2 + y) * QUART : (3 + y) * QUART].astype(BF)
                if slots < 2:
                    o[:, cols] = ob
                    dq[:, cols] = dqb
                else:
                    o[0 : 2 * NLAT, cols] = ob[0 : 2 * NLAT]
                    dq[0 : 2 * NLAT, cols] = dqb[0 : 2 * NLAT]
                for z in range(slots):
                    ox, dqx, dk, dv, gx = done.pop(0)
                    if slots == 1:
                        xo[0, :, cols] = ox
                        xo[1, :, cols] = dqx
                    else:
                        rows = slice((2 + z) * NLAT, (3 + z) * NLAT)
                        o[rows, cols] = ob[rows] + ox
                        dq[rows, cols] = dqb[rows] + dqx
                    for h in range(2):
                        rows = slice(h * 2 * QUART, (h + 1) * 2 * QUART)
                        grads[2 * z + h][:, wk] = dk[rows].astype(BF)
                        grads[2 * z + h][:, wv] = dv[rows].astype(BF)
                    gs = gs + gx
                gacc[pl.ds(c * GRP + n, 1), :] = gs

    @pl.when(source >= 0)
    def _():
        work(1)

    @pl.when(hot)
    def _():
        work(2)

    @pl.when((source < 0) & jnp.logical_not(hot))
    def _():
        work(0)

    @pl.when(c == pl.num_programs(0) - 1)
    def _():
        gate[...] = jnp.sum(gacc[...].T, axis=0, keepdims=True)


def pair_kernel(pay, got, gate, dst):
    for d in range(16):
        dst[d, :, 0:COLS] = (pay[d] + got[d].astype(F32)).astype(BF)
    gates = split3(gate[...])
    for d in range(16):
        dst[d, :, COLS:WIDE] = gates


def collect_kernel(got, dst, gate):
    total = got[0].astype(F32)
    for p in range(1, 16):
        total += got[p].astype(F32)
    gate[...] = jnp.sum(total[:, COLS:WIDE], axis=0, keepdims=True)
    val = total[:, 0:COLS].astype(BF)
    for j in range(8):
        dst[j] = val


def sort_kernel(here, r0, r1, r2, r3, own, give, sems):
    chip = here[0] // 2
    step = jnp.where(chip // 4 % 2 == 0, chip % 2, chip % 4)
    for s, r in enumerate((r2, r3, r0, r1)):

        @pl.when(step == s)
        def _():
            first = pltpu.make_async_copy(r.at[pl.ds(0, QUART)], own, sems.at[0])
            second = pltpu.make_async_copy(r.at[pl.ds(QUART, QUART)], give, sems.at[1])
            first.start()
            second.start()
            first.wait()
            second.wait()


def assemble_kernel(here, lead_ref, got, own, given, dst):
    ctx, lead = here[0], lead_ref[0]
    image = ctx // 4
    low = (image > 3) & (image < 6) | (image < lead)
    held = low == (ctx % 2 == 0)

    @pl.when(image == lead)
    def _():
        for i in range(8):
            dst[:, i * COLS : (i + 1) * COLS] = got[i]

    @pl.when((image != lead) & held)
    def _():
        dst[...] = own[...]

    @pl.when((image != lead) & jnp.logical_not(held))
    def _():
        dst[...] = given[...]


def merge_kernel(here, images, lead_ref, o_in, dq_in, r0, r1, o, dq, buf, sems):
    del o_in, dq_in
    ctx, lead = here[0], lead_ref[0]

    def odd(s):
        return sends(ctx, s) & (images[step_block(ctx, s)] != lead)

    def load(s):
        return pltpu.make_async_copy((r0, r1)[s], buf.at[s], sems.at[s, 0])

    def stores(s):
        rows = pl.ds(pl.multiple_of(step_block(ctx, s) * NLAT, NLAT), NLAT)
        return (
            pltpu.make_async_copy(buf.at[s, 0], o.at[rows], sems.at[s, 1]),
            pltpu.make_async_copy(buf.at[s, 1], dq.at[rows], sems.at[s, 2]),
        )

    for s in range(2):

        @pl.when(odd(s))
        def _():
            load(s).start()

    for s in range(2):

        @pl.when(odd(s))
        def _():
            load(s).wait()
            for copy in stores(s):
                copy.start()

    for s in range(2):

        @pl.when(odd(s))
        def _():
            for copy in stores(s):
                copy.wait()


VM = pl.BlockSpec(memory_space=pltpu.VMEM)
SM = pl.BlockSpec(memory_space=pltpu.SMEM)
HBM = pl.BlockSpec(memory_space=pltpu.HBM)
ANY = pl.BlockSpec(memory_space=pl.ANY)
LIMIT = 48 * 1024 * 1024
SMALL = 16 * 1024 * 1024


def shape(*dims, dtype=BF):
    return jax.ShapeDtypeStruct(dims, dtype)


def call(kernel, name, out_shape, in_specs, out_specs, cost=(0, 0), limit=SMALL, **more):
    estimate = pl.CostEstimate(flops=cost[0], bytes_accessed=cost[1], transcendentals=0)
    params = pltpu.CompilerParams(vmem_limit_bytes=limit)
    return pl.pallas_call(
        kernel,
        name=name,
        out_shape=out_shape,
        in_specs=in_specs,
        out_specs=out_specs,
        compiler_params=params,
        cost_estimate=estimate,
        **more,
    )


def body(queries, latent_kv, media, gate, grad_out):
    q, g, kv_rows = queries[0], grad_out[0], latent_kv[0]
    tokens, width = q.shape
    here = lax.axis_index(CTX).astype(jnp.int32)[None]
    images = media[0]
    swap = [(0, 1), (1, 0)]

    packed = call(
        pack_kernel,
        "pack",
        [shape(2, NLAT, width)] * 2,
        [SM, HBM, HBM],
        [HBM] * 2,
        limit=62 * 1024 * 1024,
        scratch_shapes=[
            pltpu.VMEM((2, 2, NLAT, width), BF),
            pltpu.SemaphoreType.DMA((2, 2, 2)),
        ],
    )(here, q, g)
    chunks = call(chunk_kernel, "chunk", shape(8, QUART, WIDE), [SM, VM], VM)(images, kv_rows)
    mixed = lax.all_to_all(chunks, IMG, 0, 0, tiled=True)
    sent = [lax.ppermute(packed[s], CTX, BLOCK_PAIRS[s]) for s in range(2)]
    chip_rows = call(half_kernel, "half", shape(2 * QUART, 2 * width), [VM, VM], VM)(
        kv_rows, lax.ppermute(kv_rows, "c", swap)
    )
    lent = [lax.ppermute(chip_rows, CTX, latent_pairs(s)) for s in range(4)]

    spread, lead = call(
        spread_kernel,
        "spread",
        [shape(16, QUART, COLS), shape(1, dtype=jnp.int32)],
        [VM],
        [VM, SM],
    )(mixed)
    mine = lax.all_to_all(spread, CHIP, 0, 0, tiled=True).reshape(2, 4, 2, QUART, COLS)
    other = lax.ppermute(mine, "c", swap)

    tanh_gate = jnp.tanh(gate)
    wide = pl.BlockSpec((tokens, COLS), lambda c: (0, c))
    half = pl.BlockSpec((2, 1, 2, QUART, COLS), lambda c: (0, c, 0, 0, 0))
    o, dq, xo, pay, opay, y0, y1, y2, y3, gpart = call(
        attention_kernel,
        "attention",
        [
            shape(tokens, width),
            shape(tokens, width),
            shape(2, NLAT, width),
            shape(16, QUART, COLS, dtype=F32),
            shape(16, QUART, COLS),
            *[shape(2 * QUART, 2 * width)] * 4,
            shape(1, HS, dtype=F32),
        ],
        [SM, SM, SM, SM, wide, wide, half, half, *[VM] * 4, HBM, HBM],
        [wide, wide, pl.BlockSpec((2, NLAT, COLS), lambda c: (0, 0, c)), *[VM] * 7],
        grid=(4,),
        limit=LIMIT,
        scratch_shapes=[
            pltpu.VMEM((2, NLAT, width), BF),
            pltpu.VMEM((HS, HS), F32),
            pltpu.SemaphoreType.DMA,
        ],
    )(here, images, lead, tanh_gate, q, g, mine, other, *lent, *sent)

    gpart = gpart + lax.ppermute(gpart, "dp", [(s, s ^ 1) for s in range(8)])
    theirs = lax.ppermute(opay, "c", swap)
    paired = call(pair_kernel, "pair", shape(16, QUART, WIDE), [VM, VM, VM], VM)(
        pay, theirs, gpart
    )
    parts = lax.all_to_all(paired, CHIP, 0, 0, tiled=True)
    owned = [lax.ppermute(y, CTX, back(latent_pairs(s))) for s, y in enumerate((y0, y1, y2, y3))]
    own, give = call(
        sort_kernel,
        "sort",
        [shape(QUART, 2 * width)] * 2,
        [SM, *[ANY] * 4],
        [VM, VM],
        scratch_shapes=[pltpu.SemaphoreType.DMA((2,))],
    )(here, *owned)
    given = lax.ppermute(give, "c", swap)
    ready = [lax.ppermute(xo, CTX, back(BLOCK_PAIRS[s])) for s in range(2)]
    summed, gates = call(
        collect_kernel,
        "collect",
        [shape(8, QUART, COLS), shape(1, HS, dtype=F32)],
        [VM],
        [VM, VM],
    )(parts)
    gates = gates + lax.ppermute(gates, "c", swap)
    for flip in (2, 7):
        gates = gates + lax.ppermute(gates, "dp", [(s, s ^ flip) for s in range(8)])
    final = lax.all_to_all(summed, IMG, 0, 0, tiled=True)
    latent_grad = call(
        assemble_kernel, "assemble", shape(QUART, 2 * width), [SM, SM, VM, VM, VM], VM
    )(here, lead, final, own, given)
    o, dq = call(
        merge_kernel,
        "merge",
        [shape(tokens, width)] * 2,
        [SM, SM, SM, *[ANY] * 4],
        [ANY, ANY],
        scratch_shapes=[
            pltpu.VMEM((2, 2, NLAT, width), BF),
            pltpu.SemaphoreType.DMA((2, 3)),
        ],
        input_output_aliases={3: 0, 4: 1},
    )(here, images, lead, o, dq, *ready)
    gate_grad = (1.0 - tanh_gate * tanh_gate) * gates[0, :HEADS]
    return o[None], dq[None], latent_grad[None], gate_grad


def solution(mesh):
    fine = Mesh(mesh.devices.reshape(8, 4, 2, 2, 2), ("dp", "x", "yh", "yl", "c"))
    wide = P("dp", CTX, None)
    return jax.shard_map(
        body,
        mesh=fine,
        in_specs=(wide, wide, P("dp", CTX), P(), wide),
        out_specs=(wide, wide, wide, P()),
        check_vma=False,
    )
```
